32 devices in a mesh: expert: 16 (over z, x, core), hidden: 2 (over y).
Axes of the slice: x: 2, y: 2, z: 4, core: 2. Of those that a mesh axis runs over, the one named last changes fastest.
Arguments:
- swap_pairs: int32 [8, 2], replicated, may hold values from 0 to 15, as said below
- expert_ids: int32 [2048, 2], P('expert'), may hold values from 0 to 15, all different within a row; in each aligned block of 128 rows (0 to 127, 128 to 255, ...) at most 32 rows name the same one
- route_weights: float32 [2048, 2], P('expert'), may hold values from 0.05 to 0.6
- gate_up: bfloat16 [2048, 2, 2, 256], P('expert', None, None, 'hidden'), may hold values from -6 to 6
- grad_out: bfloat16 [2048, 3584], P('expert', 'hidden'), may hold values from -6 to 6
- down_weight: bfloat16 [16, 256, 3584], P('expert', 'hidden'), may hold values from -0.375 to 0.375
- first_moment: bfloat16 [16, 256, 3584], P('expert', 'hidden'), may hold values from -4 to 4
- second_moment: bfloat16 [16, 256, 3584], P('expert', 'hidden'), may hold values from 0.049804688 to 1
Outputs:
- combined: bfloat16 [2048, 3584], P('expert', 'hidden')
- grad_gate_up: bfloat16 [2048, 2, 2, 256], P('expert', None, None, 'hidden')
- adam_step: bfloat16 [16, 256, 3584], P('expert', 'hidden')
The draws below stay inside these ranges and needn't reach their ends.
Inputs may be any that keep to these rules, and one draw needn't show every extreme that they name: `swap_pairs`: every place 0 .. 15 appears exactly once in the list. `expert_ids`: A row's 2 experts are distinct; in each aligned block of 128 rows (the rows of one device) no expert is named more than 32 times, a bound that some block reaches.
All inputs are finite; a program needn't handle non-finite values.
Results may differ from the reference program's by a relative error of at most 0.017.
Values may be sent and summed in bfloat16 or wider, within the bound.
No kernel may reach another device: no remote copies, remote signals or barrier semaphores. Data moves between devices by JAX's collectives and lax.ppermute only.
A program may use at most 128 MiB of HBM per device.

```python
import math
import jax
import jax.numpy as jnp
import numpy as np
from jax import lax

D = 3584
HID_DEV = 128
TOP = 2
TOK_DEV = 128
EXPERTS = 16
HID = 256
TOKENS = 2048
CAP = 32
NSWAP = 8
N_HIDDEN = 2


def draw_swap_pairs(key, part):
    shuffled = jax.random.permutation(key, EXPERTS)
    return shuffled[:2 * NSWAP].reshape(NSWAP, 2).astype(jnp.int32)


def levels(rng, shape, cuts, low, largest):
    loudness, own = 1.0, jax.random.fold_in(rng, 6)
    for axis_at, parts in cuts:
        heights = jnp.exp(jax.random.uniform(jax.random.fold_in(own, axis_at), (parts,), jnp.float32, low / len(cuts), largest / len(cuts)))
        loudness = loudness * jnp.repeat(heights, shape[axis_at] // parts).reshape([-1 if axis == axis_at else 1 for axis in range(len(shape))])
    return loudness


def deal_out(own_key, own, number, rows, number_of, top, limit, slope):
    ranking = jax.random.permutation(own_key, number_of)
    packed, common = shares(number_of, rows * top, limit, slope, True), shares(number_of, rows * top, limit, slope, False)
    places = jnp.arange(number_of)

    def named(tallies, rotation):
        used = int((tallies > 0).sum())
        fixed = max(1, used // 4)
        moved = fixed + (places - fixed + rotation * (used - fixed)) % max(1, number_of - fixed)
        return jnp.zeros((number_of,), jnp.int32).at[ranking[jnp.where(places < fixed, places, moved)]].set(jnp.asarray(tallies, jnp.int32))

    tallies = jnp.where(number % 4 == 0, named(packed, number // 4), named(common, number - number // 4 - 1))
    mixed = jax.random.permutation(jax.random.fold_in(own, 3), number_of)
    giver, taker = mixed[0:number_of // 2 * 2:2], mixed[1:number_of // 2 * 2:2]
    margin = jnp.minimum(tallies[giver] - 1, limit - tallies[taker]) // 2
    margin = jnp.where((giver == ranking[0]) | (taker == ranking[0]) | (tallies[taker] == 0), 0, jnp.maximum(margin, 0))
    moved = jax.random.randint(jax.random.fold_in(own, 4), (number_of // 2,), 0, 1 << 20) % (margin + 1)
    tallies = tallies.at[giver].add(-moved).at[taker].add(moved)
    members = jnp.searchsorted(jnp.cumsum(tallies), jnp.arange(rows * top), side="right").astype(jnp.int32)
    grid = members.reshape(top, rows).T
    grid = grid[jax.random.permutation(jax.random.fold_in(own, 1), rows)]
    rotation = jax.random.randint(jax.random.fold_in(own, 2), (rows, 1), 0, top)
    return jnp.take_along_axis(grid, (jnp.arange(top)[None, :] + rotation) % top, axis=1)


def shares(amount, total, reach, lean, full):
    portions = [(1 << 20) // math.isqrt(rank ** lean) + 1 for rank in range(1, amount + 1)]
    largest = reach if full else min(reach, max(-(-total // amount), total * portions[0] // sum(portions)))
    least = 1 if total - largest >= amount - 1 else 0
    given, spare = [largest] + [least] * (amount - 1), total - largest - least * (amount - 1)
    while spare > 0:
        free = [i for i in range(1, amount) if given[i] < largest] or [i for i in range(1, amount) if given[i] < reach]
        pool, left = sum([portions[i] for i in free]), spare
        for i in free:
            more = min(reach - given[i], max(1, left * portions[i] // pool), spare)
            given[i] = given[i] + more
            spare = spare - more
    return np.array(given)


def noise(own_key, shape, scale, most, pieces=(), kind=jnp.bfloat16):
    level = levels(own_key, shape, pieces, -0.22, 0.18) if pieces else 1.0
    drawn = jax.random.normal(own_key, shape, jnp.float32) * scale * level
    return jnp.minimum(jnp.maximum(drawn, -most), most).astype(kind)


def setup_inputs(seed: int = 0) -> dict:
    keys = jax.random.split(jax.random.key(seed), 9)
    swap_pairs = draw_swap_pairs(jax.random.fold_in(keys[8], 71), 0)
    expert_ids_keys = jax.random.split(jax.random.fold_in(keys[1], 1), TOKENS // TOK_DEV)
    expert_ids_turns = jax.random.permutation(jax.random.fold_in(keys[1], 3), TOKENS // TOK_DEV)
    expert_ids = jax.vmap(lambda own, number: deal_out(jax.random.fold_in(keys[1], 2), own, number, TOK_DEV, EXPERTS, TOP, CAP, 2))(expert_ids_keys, expert_ids_turns).reshape((TOKENS, TOP))
    route_weights = jnp.clip(0.05 + 0.55 * jax.random.uniform(keys[2], (TOKENS, TOP), jnp.float32) ** levels(keys[2], (TOKENS, TOP), ((0, 16),), -0.2, 0.2), 0.05, 0.6)
    gate_up = noise(keys[3], (TOKENS, TOP, 2, HID), 1.0, 6.0, ((0, 16), (3, 2)))
    grad_out = noise(keys[4], (TOKENS, D), 1.0, 6.0, ((0, 16), (1, 2)))
    down_weight = noise(keys[5], (EXPERTS, HID, D), HID ** -0.5, 0.375, ((0, 16), (1, 2)))
    first_moment = noise(keys[6], (EXPERTS, HID, D), 0.5, 4.0, ((0, 16), (1, 2)))
    second_moment = jnp.clip(jnp.exp(math.log(1.0) - 2.9996462 * jax.random.uniform(keys[7], (EXPERTS, HID, D), jnp.float32) ** levels(keys[7], (EXPERTS, HID, D), ((0, 16), (1, 2)), -0.2, 0.2)), 0.049804688, 1.0).astype(jnp.bfloat16)
    return {"swap_pairs": swap_pairs, "expert_ids": expert_ids, "route_weights": route_weights, "gate_up": gate_up, "grad_out": grad_out, "down_weight": down_weight, "first_moment": first_moment, "second_moment": second_moment}


first_decay = 0.9
second_decay = 0.95
adam_epsilon = 1e-08

def partner_table(swap_pairs, places):
    column = jnp.arange(places, dtype=jnp.int32)
    left = swap_pairs[:, 0].astype(jnp.int32)
    right = swap_pairs[:, 1].astype(jnp.int32)
    moved = jnp.where(left[:, None] == column[None, :], right[:, None] - column[None, :], 0)
    moved = moved + jnp.where(right[:, None] == column[None, :], left[:, None] - column[None, :], 0)
    return (column + lax.optimization_barrier(jnp.sum(moved, axis=0))).astype(jnp.int32)

def reference(swap_pairs, expert_ids, route_weights, gate_up, grad_out, down_weight, first_moment, second_moment):
    partner = partner_table(swap_pairs, EXPERTS)
    flat_ids = expert_ids.reshape(-1).astype(jnp.int32)
    choices = flat_ids.shape[0]
    sorted_order = jnp.argsort(flat_ids, stable=True).astype(jnp.int32)
    column = jnp.arange(EXPERTS, dtype=jnp.int32)
    counts = lax.optimization_barrier(jnp.sum((flat_ids[:, None] == column[None, :]).astype(jnp.int32), axis=0))
    starts = (jnp.cumsum(counts) - counts).astype(jnp.int32)
    slot_limit = EXPERTS * CAP
    lane_index = jnp.arange(slot_limit, dtype=jnp.int32)
    act_table = gate_up.reshape(choices, 2 * HID)
    weight_flat = route_weights.reshape(-1)

    def one_expert(totals, expert):
        mixed_total, grad_total = totals
        is_valid = lane_index < counts[expert]
        picked = jnp.take(sorted_order, jnp.where(is_valid, starts[expert] + lane_index, 0).astype(jnp.int32)).astype(jnp.int32)
        token_row = (picked // TOP).astype(jnp.int32)
        act_pick = jnp.where(is_valid[:, None], jnp.take(act_table, picked, axis=0), jnp.zeros((), act_table.dtype))
        gate_pre = act_pick[:, :HID].astype(jnp.float32)
        up_pre = act_pick[:, HID:].astype(jnp.float32)
        sigmoid_gate = jax.nn.sigmoid(gate_pre)
        silu_gate = gate_pre * sigmoid_gate
        hidden = (silu_gate * up_pre).astype(jnp.bfloat16)
        factor = jnp.where(is_valid, jnp.take(weight_flat, picked), jnp.zeros((), jnp.float32))
        scaled = (factor[:, None] * jnp.take(grad_out, token_row, axis=0).astype(jnp.float32)).astype(jnp.bfloat16)
        weight = lax.dynamic_index_in_dim(down_weight, expert, 0, keepdims=False)
        grouped = jnp.einsum('rjh,jhd->jrd', hidden.reshape(slot_limit, N_HIDDEN, HID_DEV).astype(jnp.float32), weight.reshape(N_HIDDEN, HID_DEV, D).astype(jnp.float32))
        grouped = lax.optimization_barrier(grouped.astype(jnp.bfloat16))
        summed = lax.optimization_barrier(jnp.sum(grouped.astype(jnp.float32), axis=0))
        mixed_total = mixed_total.at[token_row].add(factor[:, None] * summed)
        grad_hidden = jnp.dot(scaled, weight.T, preferred_element_type=jnp.float32)
        grad_gate = grad_hidden * up_pre * sigmoid_gate * (1.0 + gate_pre * (1.0 - sigmoid_gate))
        grad_up = grad_hidden * silu_gate
        grad_rows = jnp.concatenate([grad_gate, grad_up], axis=1).astype(jnp.bfloat16)
        grad_rows = jnp.where(is_valid[:, None], grad_rows, jnp.zeros((), grad_rows.dtype))
        grad_total = grad_total.at[picked].add(grad_rows)
        grad_weight = jnp.dot(hidden.T, scaled, preferred_element_type=jnp.float32)
        first_here = lax.dynamic_index_in_dim(first_moment, expert, 0, keepdims=False).astype(jnp.float32)
        second_here = lax.dynamic_index_in_dim(second_moment, expert, 0, keepdims=False).astype(jnp.float32)
        first_new = first_decay * first_here + (1.0 - first_decay) * grad_weight
        second_new = second_decay * second_here + (1.0 - second_decay) * grad_weight * grad_weight
        update = (first_new / (jnp.sqrt(second_new) + adam_epsilon)).astype(jnp.bfloat16)
        return ((mixed_total, grad_total), update)
    initial = (jnp.zeros((TOKENS, D), jnp.float32), jnp.zeros((choices, 2 * HID), jnp.bfloat16))
    totals, updates = lax.scan(one_expert, initial, jnp.arange(EXPERTS, dtype=jnp.int32))
    combined = totals[0].astype(jnp.bfloat16)
    grad_gate_up = totals[1].reshape(TOKENS, TOP, 2, HID)
    adam_step = jnp.take(updates, partner, axis=0)
    return (combined, grad_gate_up, adam_step)
```

```python
import functools
import jax
import jax.numpy as jnp
from jax import lax
from jax.experimental import pallas as pl
from jax.experimental.pallas import tpu as pltpu
from jax.sharding import PartitionSpec as P

first_decay = 0.9
second_decay = 0.95
adam_epsilon = 1e-08


def partner_table(swap_pairs, places):
    column = jnp.arange(places, dtype=jnp.int32)
    left = swap_pairs[:, 0]
    right = swap_pairs[:, 1]
    moved = jnp.where(left[:, None] == column[None, :], right[:, None] - column[None, :], 0)
    moved = moved + jnp.where(right[:, None] == column[None, :], left[:, None] - column[None, :], 0)
    return column + jnp.sum(moved, axis=0)


def relocate_state(weight_here, first_here, second_here, partner):
    places = partner.shape[0]
    shape_here = weight_here.shape
    spread = (
        lax.all_to_all(
            weight_here.reshape(places, -1), "expert", split_axis=0, concat_axis=0, tiled=True
        ),
        lax.all_to_all(
            first_here.reshape(places, -1), "expert", split_axis=0, concat_axis=0, tiled=True
        ),
        lax.all_to_all(
            second_here.reshape(places, -1), "expert", split_axis=0, concat_axis=0, tiled=True
        ),
    )
    ordered = tuple((jnp.take(member, partner, axis=0) for member in spread))
    collected = (
        lax.all_to_all(ordered[0], "expert", split_axis=0, concat_axis=0, tiled=True),
        lax.all_to_all(ordered[1], "expert", split_axis=0, concat_axis=0, tiled=True),
        lax.all_to_all(ordered[2], "expert", split_axis=0, concat_axis=0, tiled=True),
    )
    return tuple((member.reshape(shape_here) for member in collected))


def slot_numbers(destination, places, capacity):
    column = jnp.arange(places, dtype=jnp.int32)
    one_hot = (destination[:, None] == column[None, :]).astype(jnp.int32)
    before = jnp.cumsum(one_hot, axis=0) - one_hot
    earlier_count = jnp.sum(before * one_hot, axis=1)
    return destination * capacity + earlier_count


def general_local(
    swap_pairs,
    expert_ids,
    route_weights,
    gate_up,
    grad_out,
    down_weight,
    first_moment,
    second_moment,
):
    places = lax.axis_size("expert")
    tok_count, top_count = expert_ids.shape
    hid_dev = down_weight.shape[1]
    capacity = 2 * tok_count * top_count // places
    total_slots = places * capacity
    choice_count = tok_count * top_count
    partner = partner_table(swap_pairs, places)
    weight_here = down_weight[0]
    first_here = first_moment[0]
    second_here = second_moment[0]
    flat_ids = expert_ids.reshape(-1)
    column = jnp.arange(places, dtype=jnp.int32)
    weight_here, first_here, second_here = relocate_state(
        weight_here, first_here, second_here, partner
    )
    destination = jnp.sum(
        jnp.where(flat_ids[:, None] == column[None, :], partner[None, :], 0), axis=1
    )
    slot_index = slot_numbers(destination, places, capacity)
    choice_acts = gate_up.reshape(choice_count, 2 * hid_dev)
    scaled = (route_weights[:, :, None] * grad_out[:, None, :].astype(jnp.float32)).astype(
        jnp.bfloat16
    )
    scaled = scaled.reshape(choice_count, grad_out.shape[1])
    send_acts = jnp.zeros((total_slots, 2 * hid_dev), jnp.bfloat16).at[slot_index].set(choice_acts)
    send_grads = (
        jnp.zeros((total_slots, grad_out.shape[1]), jnp.bfloat16).at[slot_index].set(scaled)
    )
    recv_acts, recv_grads = (
        lax.all_to_all(
            send_acts.reshape(places, capacity, 2 * hid_dev),
            "expert",
            split_axis=0,
            concat_axis=0,
            tiled=True,
        ),
        lax.all_to_all(
            send_grads.reshape(places, capacity, grad_out.shape[1]),
            "expert",
            split_axis=0,
            concat_axis=0,
            tiled=True,
        ),
    )
    recv_acts = recv_acts.reshape(total_slots, 2 * hid_dev)
    recv_grads = recv_grads.reshape(total_slots, grad_out.shape[1])
    gate_pre = recv_acts[:, :hid_dev].astype(jnp.float32)
    up_pre = recv_acts[:, hid_dev:].astype(jnp.float32)
    sigmoid_gate = jax.nn.sigmoid(gate_pre)
    silu_gate = gate_pre * sigmoid_gate
    hidden = (silu_gate * up_pre).astype(jnp.bfloat16)
    partial_value = jnp.dot(hidden, weight_here, preferred_element_type=jnp.float32)
    summed = lax.psum_scatter(
        partial_value.astype(jnp.bfloat16), "hidden", scatter_dimension=1, tiled=True
    ).astype(jnp.float32)
    returned = lax.all_to_all(
        summed.reshape(places, capacity, summed.shape[1]).astype(jnp.bfloat16),
        "expert",
        split_axis=0,
        concat_axis=0,
        tiled=True,
    ).astype(jnp.float32)
    per_choice = jnp.take(returned.reshape(total_slots, summed.shape[1]), slot_index, axis=0)
    per_choice = per_choice.reshape(tok_count, top_count, summed.shape[1])
    combined = jnp.einsum("tk,tkd->td", route_weights, per_choice).astype(jnp.bfloat16)
    portion = lax.all_gather(recv_grads, "hidden", axis=1, tiled=True)
    grad_hidden = lax.dot_general(
        portion, weight_here, (((1,), (1,)), ((), ())), preferred_element_type=jnp.float32
    )
    product_block = lax.dot_general(
        hidden, portion, (((0,), (0,)), ((), ())), preferred_element_type=jnp.float32
    )
    grad_weight = product_block
    grad_hidden, grad_weight = (grad_hidden, grad_weight)
    grad_gate = grad_hidden * up_pre * sigmoid_gate * (1.0 + gate_pre * (1.0 - sigmoid_gate))
    grad_up = grad_hidden * silu_gate
    grad_rows = jnp.concatenate([grad_gate, grad_up], axis=1).astype(jnp.bfloat16)
    returned_grads = lax.all_to_all(
        grad_rows.reshape(places, capacity, 2 * hid_dev),
        "expert",
        split_axis=0,
        concat_axis=0,
        tiled=True,
    )
    grad_gate_up = jnp.take(returned_grads.reshape(total_slots, 2 * hid_dev), slot_index, axis=0)
    grad_gate_up = grad_gate_up.reshape(tok_count, top_count, 2, hid_dev)
    first_new = first_decay * first_here.astype(jnp.float32) + (1.0 - first_decay) * grad_weight
    second_new = (
        second_decay * second_here.astype(jnp.float32)
        + (1.0 - second_decay) * grad_weight * grad_weight
    )
    update = (first_new / (jnp.sqrt(second_new) + adam_epsilon)).astype(jnp.bfloat16)
    return (combined, grad_gate_up, update[None])


bf16 = jnp.bfloat16
f32 = jnp.float32
KERNEL_PARAMS = pltpu.CompilerParams(vmem_limit_bytes=40 * 1024 * 1024)


def whole_call(body, out_shape, name, cost=None):
    return pl.pallas_call(body, out_shape=out_shape, name=name, compiler_params=KERNEL_PARAMS)


def quarters_body(order_ref, *refs):
    outs = refs[-1]
    for k, ref in enumerate(refs[:-1]):
        outs[0, 0, k] = ref[...]


def split_quarters(order, members, wide):
    rows = members[0].shape[0]
    return pl.pallas_call(
        quarters_body,
        grid_spec=pltpu.PrefetchScalarGridSpec(
            num_scalar_prefetch=1,
            grid=(2, 2),
            in_specs=[
                pl.BlockSpec((rows, wide), lambda a, b, order: (0, order[2 * a + b]))
                for _ in members
            ],
            out_specs=pl.BlockSpec(
                (1, 1, len(members), rows, wide), lambda a, b, order: (a, b, 0, 0, 0)
            ),
        ),
        out_shape=jax.ShapeDtypeStruct((2, 2, len(members), rows, wide), members[0].dtype),
        name="split_quarters",
        compiler_params=KERNEL_PARAMS,
    )(order, *members)


def hidden_body(own_ref, other_ref, hidden_ref):
    tok = own_ref.shape[0]
    units = own_ref.shape[1] // 4
    for side, ref in enumerate((own_ref, other_ref)):
        for choice in range(2):
            at = 2 * choice * units
            gate = ref[:, at : at + units].astype(f32)
            up = ref[:, at + units : at + 2 * units].astype(f32)
            value = (gate * jax.nn.sigmoid(gate) * up).astype(bf16)
            hidden_ref[choice * tok : (choice + 1) * tok, side * units : (side + 1) * units] = value


def slot_choice(meta, slots, bins):
    flat = jnp.concatenate([meta[0:1, :], meta[1:2, :]], axis=1)
    count = flat.shape[1]
    column = lax.broadcasted_iota(jnp.int32, (bins, count), 0).astype(f32)
    one_hot = (flat == column).astype(f32)
    first = lax.broadcasted_iota(jnp.int32, (count, count), 0)
    second = lax.broadcasted_iota(jnp.int32, (count, count), 1)
    earlier = (first < second).astype(bf16)
    rank = jnp.dot(one_hot.astype(bf16), earlier, preferred_element_type=f32)
    slot = jnp.sum(one_hot * (rank + column * (slots // bins)), axis=0, keepdims=True)
    return slot == lax.broadcasted_iota(jnp.int32, (slots, count), 0).astype(f32)


def pack_body(meta0, meta1, hidden0, hidden1, grads0, grads1, out_ref):
    bins, _, cap, _ = out_ref.shape
    slots = bins * cap
    wide = grads0.shape[1]
    tok = grads0.shape[0]
    for block, (meta_ref, hidden_ref, grads_ref) in enumerate(
        ((meta0, hidden0, grads0), (meta1, hidden1, grads1))
    ):
        meta = meta_ref[...]
        chosen = slot_choice(meta, slots, bins)
        weights = jnp.concatenate([meta[2:3, :], meta[3:4, :]], axis=1)
        factor = jnp.sum(jnp.where(chosen, weights, 0.0), axis=1, keepdims=True)
        one_hot = chosen.astype(f32)
        by_token = (one_hot[:, :tok] + one_hot[:, tok:]).astype(bf16)
        rows = jnp.dot(by_token, grads_ref[...], preferred_element_type=f32)
        rows = (rows * factor).astype(bf16)
        out_ref[:, block, :, 0:wide] = rows.reshape(bins, cap, wide)
        acts = jnp.dot(one_hot.astype(bf16), hidden_ref[...], preferred_element_type=f32)
        out_ref[:, block, :, wide:] = acts.astype(bf16).reshape(bins, cap, -1)


def forward_body(recv_ref, own_ref, mirror_ref, out_ref):
    sources, _, rows, wide = out_ref.shape
    units = own_ref.shape[2]
    for expert, ref in enumerate((own_ref, mirror_ref)):
        total = None
        for side in range(2):
            at = wide + side * units
            acts = recv_ref[:, expert, :, at : at + units].reshape(sources * rows, units)
            part = jnp.dot(acts, ref[side, 0], preferred_element_type=f32)
            total = part if total is None else total + part
        out_ref[:, expert] = total.astype(bf16).reshape(sources, rows, wide)


def grad_hidden_body(recv_ref, own_ref, mirror_ref, keep_ref, send_ref):
    sources, _, rows, units = send_ref.shape
    wide = own_ref.shape[3]
    for expert, ref in enumerate((own_ref, mirror_ref)):
        scaled = recv_ref[:, expert, :, 0:wide].reshape(sources * rows, wide)
        for side, out_ref in enumerate((keep_ref, send_ref)):
            part = lax.dot_general(
                scaled, ref[side, 0], (((1,), (1,)), ((), ())), preferred_element_type=f32
            )
            out_ref[:, expert] = part.astype(out_ref.dtype).reshape(sources, rows, units)


def update_body(recv_ref, own_ref, mirror_ref, keep_ref, got_ref, out_ref):
    sources, _, rows, _ = recv_ref.shape
    wide = own_ref.shape[3]
    units = own_ref.shape[2]
    each = units // sources
    for expert, ref in enumerate((own_ref, mirror_ref)):
        scaled = recv_ref[:, expert, :, 0:wide].reshape(sources * rows, wide)
        for side in range(2):
            at = wide + side * units
            acts = recv_ref[:, expert, :, at : at + units].reshape(sources * rows, units)
            grad = lax.dot_general(
                acts, scaled, (((0,), (0,)), ((), ())), preferred_element_type=f32
            )
            first = first_decay * ref[side, 0].astype(f32) + (1.0 - first_decay) * grad
            second = second_decay * ref[side, 1].astype(f32) + (1.0 - second_decay) * grad * grad
            step = (first / (jnp.sqrt(second) + adam_epsilon)).astype(bf16)
            at = (2 * expert + side) * each
            out_ref[:, at : at + each, 0:wide] = step.reshape(sources, each, wide)
        total = keep_ref[:, expert] + got_ref[:, expert].astype(f32)
        at = wide + expert * units
        out_ref[:, :, at : at + units] = total.astype(bf16)


def combine_body(meta0, meta1, weights0, weights1, back_ref, own_ref, mirror_ref):
    bins, _, cap, wide = back_ref.shape
    slots = bins * cap
    tok = own_ref.shape[0]
    for block, (meta_ref, weights_ref, out_ref) in enumerate(
        ((meta0, weights0, own_ref), (meta1, weights1, mirror_ref))
    ):
        chosen = slot_choice(meta_ref[...], slots, bins).astype(f32).astype(bf16)
        rows = back_ref[:, block].reshape(slots, wide)
        total = None
        for choice in range(2):
            picked = lax.dot_general(
                chosen[:, choice * tok : (choice + 1) * tok],
                rows,
                (((0,), (0,)), ((), ())),
                preferred_element_type=f32,
            )
            part = weights_ref[:, choice : choice + 1] * picked
            total = part if total is None else total + part
        out_ref[...] = total.astype(bf16)


def pick_grads_body(meta0, meta1, recv_ref, own_ref, mirror_ref):
    sources, rows, total_wide = recv_ref.shape
    units = own_ref.shape[1]
    wide = total_wide - 2 * units
    cap = rows // 2
    slots = sources * 2 * cap
    for block, (meta_ref, out_ref) in enumerate(((meta0, own_ref), (meta1, mirror_ref))):
        chosen = slot_choice(meta_ref[...], slots, 2 * sources).astype(f32).astype(bf16)
        pieces = []
        for expert in range(2):
            at = wide + expert * units
            pieces.append(recv_ref[:, block * cap : (block + 1) * cap, at : at + units])
        table = jnp.stack(pieces, axis=1).reshape(slots, units)
        picked = lax.dot_general(
            chosen, table, (((0,), (0,)), ((), ())), preferred_element_type=f32
        )
        out_ref[...] = picked.astype(out_ref.dtype)


def gate_grads_body(acts_ref, own_ref, got_ref, out_ref):
    tok = acts_ref.shape[0]
    units = own_ref.shape[1]
    for choice in range(2):
        at = 2 * choice * units
        gate = acts_ref[:, at : at + units].astype(f32)
        up = acts_ref[:, at + units : at + 2 * units].astype(f32)
        lines = slice(choice * tok, (choice + 1) * tok)
        grad = own_ref[lines, :] + got_ref[lines, :].astype(f32)
        sigmoid = jax.nn.sigmoid(gate)
        out_ref[:, at : at + units] = (
            grad * up * sigmoid * (1.0 + gate * (1.0 - sigmoid))
        ).astype(bf16)
        out_ref[:, at + units : at + 2 * units] = (grad * (gate * sigmoid)).astype(bf16)


def route_steps_body(source_ref, line_ref, recv_ref, out_ref):
    count, each, wide = out_ref.shape
    for k in range(count):
        line = pl.multiple_of(line_ref[k] * each, each)
        out_ref[k] = recv_ref[source_ref[k], pl.ds(line, each), 0:wide]


def place_steps_body(recv_ref, out_ref):
    halves, sources, sides, each, wide = recv_ref.shape
    for half in range(halves):
        for source in range(sources):
            for side in range(sides):
                at = (side * halves + half) * wide
                out_ref[source * each : (source + 1) * each, at : at + wide] = recv_ref[
                    half, source, side
                ]


def mirrored_local(
    swap_pairs,
    expert_ids,
    route_weights,
    gate_up,
    grad_out,
    down_weight,
    first_moment,
    second_moment,
):
    places = lax.axis_size("expert")
    half = places // 2
    here = lax.axis_index("expert")
    side = lax.axis_index("hidden")
    level = here // half
    tok, top = expert_ids.shape
    units = down_weight.shape[1]
    wide = grad_out.shape[1] // 2
    cap = 2 * tok * top // places
    across = [(k, (k + half) % places) for k in range(places)]
    beside = [(0, 1), (1, 0)]
    groups = [list(range(half)), list(range(half, places))]

    def mirror(x):
        return lax.ppermute(x, "expert", across)

    def neighbour(x):
        return lax.ppermute(x, "hidden", beside)

    def exchange(x):
        return lax.all_to_all(
            x, "expert", split_axis=0, concat_axis=0, tiled=True, axis_index_groups=groups
        )

    order = jnp.stack(
        [(side ^ a) * 2 + (level ^ b) for a in range(2) for b in range(2)]
    ).astype(jnp.int32)

    grads_own = lax.dynamic_slice(grad_out, (0, level * wide), (tok, wide))
    grads_far = lax.dynamic_slice(grad_out, (0, (1 - level) * wide), (tok, wide))
    acts = gate_up.reshape(tok, 4 * units)
    raw_own = jnp.concatenate([expert_ids.T.astype(f32), route_weights.T], axis=0)
    grads_mirror = mirror(grads_far)
    raw_mirror = mirror(raw_own)
    acts_beside = neighbour(acts)

    def relative(raw):
        named = raw[:top].astype(jnp.int32)
        bins = (named % half) * 2 + ((named // half) ^ level)
        return jnp.concatenate([bins.astype(f32), raw[top:]], axis=0)

    meta_own = relative(raw_own)
    meta_mirror = relative(raw_mirror)
    hidden_own = whole_call(
        hidden_body, jax.ShapeDtypeStruct((top * tok, 2 * units), bf16), "hidden"
    )(acts, acts_beside)
    hidden_mirror = mirror(hidden_own)

    weight = split_quarters(order, (down_weight[0],), wide)
    weight_beside = neighbour(weight[1])
    weight_own = jnp.stack([weight[0, 0], weight_beside[0]])
    weight_mirror = mirror(jnp.stack([weight[0, 1], weight_beside[1]]))
    moments = split_quarters(order, (first_moment[0], second_moment[0]), wide)
    moments_beside = neighbour(moments[1])
    moments_own = jnp.stack([moments[0, 0], moments_beside[0]])
    moments_mirror = mirror(jnp.stack([moments[0, 1], moments_beside[1]]))

    packed = whole_call(
        pack_body, jax.ShapeDtypeStruct((places, 2, cap, wide + 2 * units), bf16), "pack"
    )(meta_own, meta_mirror, hidden_own, hidden_mirror, grads_own, grads_mirror)
    recv = exchange(packed.reshape(half, 4 * cap, wide + 2 * units))
    recv = recv.reshape(half, 2, 2 * cap, wide + 2 * units)

    partial_rows = whole_call(
        forward_body, jax.ShapeDtypeStruct((half, 2, 2 * cap, wide), bf16), "forward"
    )(recv, weight_own, weight_mirror)
    back = exchange(partial_rows.reshape(half, 4 * cap, wide)).reshape(places, 2, cap, wide)

    grad_keep, grad_send = whole_call(
        grad_hidden_body,
        (
            jax.ShapeDtypeStruct((half, 2, 2 * cap, units), f32),
            jax.ShapeDtypeStruct((half, 2, 2 * cap, units), bf16),
        ),
        "grad_hidden",
    )(recv, weight_own, weight_mirror)
    grad_got = neighbour(grad_send)

    steps = whole_call(
        update_body, jax.ShapeDtypeStruct((half, 2 * cap, wide + 2 * units), bf16), "update"
    )(recv, moments_own, moments_mirror, grad_keep, grad_got)
    spread = exchange(steps)

    partner = partner_table(swap_pairs, places)
    from_source = jnp.repeat(partner % half, 2)
    sides = jnp.tile(jnp.arange(2, dtype=jnp.int32), places)
    from_line = jnp.repeat((partner // half) ^ level, 2) * 2 + (sides ^ side)
    each = units // half
    smem = pl.BlockSpec(memory_space=pltpu.SMEM)
    vmem = pl.BlockSpec(memory_space=pltpu.VMEM)
    routed = pl.pallas_call(
        route_steps_body,
        in_specs=[smem, smem, vmem],
        out_specs=vmem,
        out_shape=jax.ShapeDtypeStruct((2 * places, each, wide), bf16),
        name="route_steps",
        compiler_params=KERNEL_PARAMS,
    )(from_source.astype(jnp.int32), from_line.astype(jnp.int32), spread)
    placed = lax.all_to_all(
        routed, ("expert", "hidden"), split_axis=0, concat_axis=0, tiled=True
    )

    combined_own, combined_far = whole_call(
        combine_body,
        (jax.ShapeDtypeStruct((tok, wide), bf16), jax.ShapeDtypeStruct((tok, wide), bf16)),
        "combine",
    )(meta_own, meta_mirror, route_weights, raw_mirror[top:].T, back)
    combined_mirror = mirror(combined_far)
    combined = jnp.where(
        level == 0,
        jnp.concatenate([combined_own, combined_mirror], axis=1),
        jnp.concatenate([combined_mirror, combined_own], axis=1),
    )

    picked_own, picked_far = whole_call(
        pick_grads_body,
        (
            jax.ShapeDtypeStruct((top * tok, units), f32),
            jax.ShapeDtypeStruct((top * tok, units), bf16),
        ),
        "pick_grads",
    )(meta_own, meta_mirror, spread)
    picked_mirror = mirror(picked_far)
    grad_gate_up = whole_call(
        gate_grads_body, jax.ShapeDtypeStruct((tok, 4 * units), bf16), "gate_grads"
    )(acts, picked_own, picked_mirror).reshape(gate_up.shape)

    adam_step = whole_call(
        place_steps_body, jax.ShapeDtypeStruct((units, 4 * wide), bf16), "place_steps"
    )(placed.reshape(2, half, 2, each, wide))
    return combined, grad_gate_up, adam_step[None]


def chosen_local(places, sides, *arrays):
    tok, top = arrays[1].shape
    units = arrays[5].shape[1]
    wide = arrays[4].shape[1] // 2
    cap = 2 * tok * top // places
    fits = sides == 2 and top == 2 and places % 4 == 0 and places * cap == 2 * tok * top
    fits = fits and wide % 128 == 0 and units % 128 == 0 and tok % 128 == 0 and cap % 16 == 0
    fits = fits and units % (8 * places) == 0 and 2 * cap == 4 * (units // (places // 2))
    return mirrored_local(*arrays) if fits else general_local(*arrays)


def solution(mesh):
    placed = (
        P(),
        P("expert", None),
        P("expert", None),
        P("expert", None, None, "hidden"),
        P("expert", "hidden"),
        P("expert", "hidden", None),
        P("expert", "hidden", None),
        P("expert", "hidden", None),
    )
    return jax.shard_map(
        functools.partial(chosen_local, mesh.shape["expert"], mesh.shape["hidden"]),
        mesh=mesh,
        in_specs=placed,
        out_specs=(
            P("expert", "hidden"),
            P("expert", None, None, "hidden"),
            P("expert", "hidden", None),
        ),
        check_vma=False,
    )
```

```python
import functools
import jax
import jax.numpy as jnp
from jax import lax
from jax.experimental import pallas as pl
from jax.experimental.pallas import tpu as pltpu
from jax.sharding import PartitionSpec as P

first_decay = 0.9
second_decay = 0.95
adam_epsilon = 1e-08


def partner_table(swap_pairs, places):
    column = jnp.arange(places, dtype=jnp.int32)
    left = swap_pairs[:, 0]
    right = swap_pairs[:, 1]
    moved = jnp.where(left[:, None] == column[None, :], right[:, None] - column[None, :], 0)
    moved = moved + jnp.where(right[:, None] == column[None, :], left[:, None] - column[None, :], 0)
    return column + jnp.sum(moved, axis=0)


def relocate_state(weight_here, first_here, second_here, partner):
    places = partner.shape[0]
    shape_here = weight_here.shape
    spread = (
        lax.all_to_all(
            weight_here.reshape(places, -1), "expert", split_axis=0, concat_axis=0, tiled=True
        ),
        lax.all_to_all(
            first_here.reshape(places, -1), "expert", split_axis=0, concat_axis=0, tiled=True
        ),
        lax.all_to_all(
            second_here.reshape(places, -1), "expert", split_axis=0, concat_axis=0, tiled=True
        ),
    )
    ordered = tuple((jnp.take(member, partner, axis=0) for member in spread))
    collected = (
        lax.all_to_all(ordered[0], "expert", split_axis=0, concat_axis=0, tiled=True),
        lax.all_to_all(ordered[1], "expert", split_axis=0, concat_axis=0, tiled=True),
        lax.all_to_all(ordered[2], "expert", split_axis=0, concat_axis=0, tiled=True),
    )
    return tuple((member.reshape(shape_here) for member in collected))


def slot_numbers(destination, places, capacity):
    column = jnp.arange(places, dtype=jnp.int32)
    one_hot = (destination[:, None] == column[None, :]).astype(jnp.int32)
    before = jnp.cumsum(one_hot, axis=0) - one_hot
    earlier_count = jnp.sum(before * one_hot, axis=1)
    return destination * capacity + earlier_count


def general_local(
    swap_pairs,
    expert_ids,
    route_weights,
    gate_up,
    grad_out,
    down_weight,
    first_moment,
    second_moment,
):
    places = lax.axis_size("expert")
    tok_count, top_count = expert_ids.shape
    hid_dev = down_weight.shape[1]
    capacity = 2 * tok_count * top_count // places
    total_slots = places * capacity
    choice_count = tok_count * top_count
    partner = partner_table(swap_pairs, places)
    weight_here = down_weight[0]
    first_here = first_moment[0]
    second_here = second_moment[0]
    flat_ids = expert_ids.reshape(-1)
    column = jnp.arange(places, dtype=jnp.int32)
    weight_here, first_here, second_here = relocate_state(
        weight_here, first_here, second_here, partner
    )
    destination = jnp.sum(
        jnp.where(flat_ids[:, None] == column[None, :], partner[None, :], 0), axis=1
    )
    slot_index = slot_numbers(destination, places, capacity)
    choice_acts = gate_up.reshape(choice_count, 2 * hid_dev)
    scaled = (route_weights[:, :, None] * grad_out[:, None, :].astype(jnp.float32)).astype(
        jnp.bfloat16
    )
    scaled = scaled.reshape(choice_count, grad_out.shape[1])
    send_acts = jnp.zeros((total_slots, 2 * hid_dev), jnp.bfloat16).at[slot_index].set(choice_acts)
    send_grads = (
        jnp.zeros((total_slots, grad_out.shape[1]), jnp.bfloat16).at[slot_index].set(scaled)
    )
    recv_acts, recv_grads = (
        lax.all_to_all(
            send_acts.reshape(places, capacity, 2 * hid_dev),
            "expert",
            split_axis=0,
            concat_axis=0,
            tiled=True,
        ),
        lax.all_to_all(
            send_grads.reshape(places, capacity, grad_out.shape[1]),
            "expert",
            split_axis=0,
            concat_axis=0,
            tiled=True,
        ),
    )
    recv_acts = recv_acts.reshape(total_slots, 2 * hid_dev)
    recv_grads = recv_grads.reshape(total_slots, grad_out.shape[1])
    gate_pre = recv_acts[:, :hid_dev].astype(jnp.float32)
    up_pre = recv_acts[:, hid_dev:].astype(jnp.float32)
    sigmoid_gate = jax.nn.sigmoid(gate_pre)
    silu_gate = gate_pre * sigmoid_gate
    hidden = (silu_gate * up_pre).astype(jnp.bfloat16)
    partial_value = jnp.dot(hidden, weight_here, preferred_element_type=jnp.float32)
    summed = lax.psum_scatter(
        partial_value.astype(jnp.bfloat16), "hidden", scatter_dimension=1, tiled=True
    ).astype(jnp.float32)
    returned = lax.all_to_all(
        summed.reshape(places, capacity, summed.shape[1]).astype(jnp.bfloat16),
        "expert",
        split_axis=0,
        concat_axis=0,
        tiled=True,
    ).astype(jnp.float32)
    per_choice = jnp.take(returned.reshape(total_slots, summed.shape[1]), slot_index, axis=0)
    per_choice = per_choice.reshape(tok_count, top_count, summed.shape[1])
    combined = jnp.einsum("tk,tkd->td", route_weights, per_choice).astype(jnp.bfloat16)
    portion = lax.all_gather(recv_grads, "hidden", axis=1, tiled=True)
    grad_hidden = lax.dot_general(
        portion, weight_here, (((1,), (1,)), ((), ())), preferred_element_type=jnp.float32
    )
    product_block = lax.dot_general(
        hidden, portion, (((0,), (0,)), ((), ())), preferred_element_type=jnp.float32
    )
    grad_weight = product_block
    grad_hidden, grad_weight = (grad_hidden, grad_weight)
    grad_gate = grad_hidden * up_pre * sigmoid_gate * (1.0 + gate_pre * (1.0 - sigmoid_gate))
    grad_up = grad_hidden * silu_gate
    grad_rows = jnp.concatenate([grad_gate, grad_up], axis=1).astype(jnp.bfloat16)
    returned_grads = lax.all_to_all(
        grad_rows.reshape(places, capacity, 2 * hid_dev),
        "expert",
        split_axis=0,
        concat_axis=0,
        tiled=True,
    )
    grad_gate_up = jnp.take(returned_grads.reshape(total_slots, 2 * hid_dev), slot_index, axis=0)
    grad_gate_up = grad_gate_up.reshape(tok_count, top_count, 2, hid_dev)
    first_new = first_decay * first_here.astype(jnp.float32) + (1.0 - first_decay) * grad_weight
    second_new = (
        second_decay * second_here.astype(jnp.float32)
        + (1.0 - second_decay) * grad_weight * grad_weight
    )
    update = (first_new / (jnp.sqrt(second_new) + adam_epsilon)).astype(jnp.bfloat16)
    return (combined, grad_gate_up, update[None])


bf16 = jnp.bfloat16
f32 = jnp.float32
KERNEL_PARAMS = pltpu.CompilerParams(vmem_limit_bytes=40 * 1024 * 1024)


def whole_call(body, out_shape, name):
    return pl.pallas_call(body, out_shape=out_shape, name=name, compiler_params=KERNEL_PARAMS)


def level_and_side(half):
    return lax.axis_index("expert") // half, lax.axis_index("hidden")


def columns_at(ref, index, wide):
    return ref[:, pl.ds(pl.multiple_of(index * wide, wide), wide)]


def same_index(size):
    first = lax.broadcasted_iota(jnp.int32, (size, size), 0)
    second = lax.broadcasted_iota(jnp.int32, (size, size), 1)
    return first == second


def prepare_body(acts_ref, ids_ref, weights_ref, hidden_ref, far_ref):
    tok = acts_ref.shape[0]
    units = acts_ref.shape[1] // 4
    for choice in range(2):
        at = 2 * choice * units
        gate = acts_ref[:, at : at + units].astype(f32)
        up = acts_ref[:, at + units : at + 2 * units].astype(f32)
        value = (gate * jax.nn.sigmoid(gate) * up).astype(bf16)
        hidden_ref[choice * tok : (choice + 1) * tok, :] = value
        far_ref[choice * tok : (choice + 1) * tok, :] = value
    weights = weights_ref[...]
    high = weights.astype(bf16)
    middle = (weights - high.astype(f32)).astype(bf16)
    low = (weights - high.astype(f32) - middle.astype(f32)).astype(bf16)
    unit = same_index(tok).astype(f32).astype(bf16)
    pieces = [
        lax.dot_general(piece, unit, (((0,), (0,)), ((), ())), preferred_element_type=f32)
        for piece in (ids_ref[...].astype(f32).astype(bf16), high, middle, low)
    ]
    blank = jnp.zeros((16 - 8, tok), f32)
    far_ref[2 * tok : 2 * tok + 16, :] = jnp.concatenate(pieces + [blank], axis=0).astype(bf16)


def split_body(*refs):
    out_ref = refs[-1]
    side = lax.axis_index("hidden")
    for k, ref in enumerate(refs[:-1]):
        out_ref[k] = columns_at(ref, 1 - side, ref.shape[1] // 2)


def read_meta(ref):
    tok = ref.shape[1]
    meta = ref[2 * tok : 2 * tok + 16, :].astype(f32)
    ids = jnp.concatenate([meta[0:1, :], meta[1:2, :]], axis=1)
    weights = [
        meta[2 + k : 3 + k, :] + meta[4 + k : 5 + k, :] + meta[6 + k : 7 + k, :] for k in range(2)
    ]
    return ids, weights


def slot_choice(bin_of, bins, cap):
    count = bin_of.shape[1]
    column = lax.broadcasted_iota(jnp.int32, (bins, count), 0).astype(f32)
    one_hot = (bin_of == column).astype(f32)
    first = lax.broadcasted_iota(jnp.int32, (count, count), 0)
    second = lax.broadcasted_iota(jnp.int32, (count, count), 1)
    earlier = (first < second).astype(f32).astype(bf16)
    rank = jnp.dot(one_hot.astype(bf16), earlier, preferred_element_type=f32)
    slot = jnp.sum(one_hot * (rank + column * cap + 1.0), axis=0, keepdims=True) - 1.0
    return slot == lax.broadcasted_iota(jnp.int32, (bins * cap, count), 0).astype(f32)


def pack_body(half, acts_ref, beside_ref, *refs):
    out_ref = refs[-1]
    bins, cap, _ = out_ref.shape
    units = beside_ref.shape[1]
    grads = jnp.concatenate([ref[...] for ref in refs[:-1]], axis=0)
    tok, wide = grads.shape
    level, _ = level_and_side(half)
    ids, weights = read_meta(acts_ref)
    chosen = slot_choice(ids - (half * level).astype(f32), bins, cap)
    weights = jnp.concatenate(weights, axis=1)
    factor = jnp.sum(jnp.where(chosen, weights, 0.0), axis=1, keepdims=True)
    one_hot = chosen.astype(f32)
    by_token = (one_hot[:, :tok] + one_hot[:, tok:]).astype(bf16)
    rows = jnp.dot(by_token, grads, preferred_element_type=f32)
    out_ref[:, :, 0:wide] = (rows * factor).astype(bf16).reshape(bins, cap, wide)
    for side, ref in enumerate((acts_ref, beside_ref)):
        at = wide + side * units
        acts = jnp.dot(
            one_hot.astype(bf16), ref[0 : 2 * tok, :], preferred_element_type=f32
        )
        out_ref[:, :, at : at + units] = acts.astype(bf16).reshape(bins, cap, units)


def rows_of(ref, start, size):
    sources, cap, _ = ref.shape
    return ref[:, :, start : start + size].reshape(sources * cap, size)


def forward_body(recv_ref, far_ref, weight_ref, beside_ref, out_ref):
    sources, _, cap, wide = out_ref.shape
    units = weight_ref.shape[0]
    weights = (columns_at(weight_ref, lax.axis_index("hidden"), wide), beside_ref[0])
    for block, ref in enumerate((recv_ref, far_ref)):
        total = None
        for side, weight in enumerate(weights):
            acts = rows_of(ref, wide + side * units, units)
            part = jnp.dot(acts, weight, preferred_element_type=f32)
            total = part if total is None else total + part
        out_ref[:, block] = total.astype(bf16).reshape(sources, cap, wide)


def grad_hidden_body(recv_ref, far_ref, weight_ref, beside_ref, keep_ref, send_ref):
    _, sources, cap, units = send_ref.shape
    wide = beside_ref.shape[2]
    own = columns_at(weight_ref, lax.axis_index("hidden"), wide)
    for block, ref in enumerate((recv_ref, far_ref)):
        scaled = rows_of(ref, 0, wide)
        for weight, out_ref in ((own, keep_ref), (beside_ref[0], send_ref)):
            part = lax.dot_general(
                scaled, weight, (((1,), (1,)), ((), ())), preferred_element_type=f32
            )
            out_ref[block] = part.astype(out_ref.dtype).reshape(sources, cap, units)


def add_sides_body(keep_ref, got_ref, own_ref, far_ref):
    own_ref[...] = (keep_ref[0] + got_ref[0].astype(f32)).astype(bf16)
    far_ref[...] = (keep_ref[1] + got_ref[1].astype(f32)).astype(bf16)


def update_body(half, recv_ref, far_ref, first_ref, second_ref, *refs):
    keep_ref, send_ref = refs[-2:]
    _, units, wide = refs[0].shape
    level, here = level_and_side(half)
    narrow = wide // 2
    for side in range(2):
        for part, out_ref in ((level, keep_ref), (1 - level, send_ref)):
            columns = pl.ds(pl.multiple_of(part * narrow, narrow), narrow)
            if side == 0:
                moments = [
                    columns_at(ref, 2 * here + part, narrow) for ref in (first_ref, second_ref)
                ]
            else:
                moments = [ref[0, :, columns] for ref in refs[:-2]]
            grad = None
            for ref in (recv_ref, far_ref):
                sources, cap, _ = ref.shape
                more = lax.dot_general(
                    rows_of(ref, wide + side * units, units),
                    ref[:, :, columns].reshape(sources * cap, narrow),
                    (((0,), (0,)), ((), ())),
                    preferred_element_type=f32,
                )
                grad = more if grad is None else grad + more
            first = first_decay * moments[0].astype(f32) + (1.0 - first_decay) * grad
            second = second_decay * moments[1].astype(f32)
            second = second + (1.0 - second_decay) * grad * grad
            out_ref[side] = (first / (jnp.sqrt(second) + adam_epsilon)).astype(bf16)


def stack_body(step_ref, far_step_ref, rows_ref, far_rows_ref, out_ref):
    sources = out_ref.shape[0]
    _, units, narrow = step_ref.shape
    cap = rows_ref.shape[1]
    each = units // sources
    for expert, (steps, rows) in enumerate(((step_ref, rows_ref), (far_step_ref, far_rows_ref))):
        for side in range(2):
            at = (2 * expert + side) * each
            out_ref[:, at : at + each, 0:narrow] = steps[side].reshape(sources, each, narrow)
        out_ref[:, expert * cap : (expert + 1) * cap, narrow:] = rows[...]


def combine_body(half, acts_ref, far_acts_ref, back_ref, own_ref, far_ref):
    bins, _, cap, wide = back_ref.shape
    tok = own_ref.shape[0]
    level, _ = level_and_side(half)
    diagonal = same_index(tok)
    for block, (ref, out_ref) in enumerate(((acts_ref, own_ref), (far_acts_ref, far_ref))):
        ids, weights = read_meta(ref)
        chosen = slot_choice(ids - (half * level).astype(f32), bins, cap)
        chosen = chosen.astype(f32).astype(bf16)
        rows = back_ref[:, block].reshape(bins * cap, wide)
        total = None
        for choice in range(2):
            picked = lax.dot_general(
                chosen[:, choice * tok : (choice + 1) * tok],
                rows,
                (((0,), (0,)), ((), ())),
                preferred_element_type=f32,
            )
            upright = jnp.sum(
                jnp.where(diagonal, weights[choice], 0.0), axis=1, keepdims=True
            )
            part = upright * picked
            total = part if total is None else total + part
        out_ref[...] = total.astype(out_ref.dtype)


def add_halves_body(own_ref, far_ref, out_ref):
    out_ref[...] = (own_ref[...] + far_ref[...].astype(f32)).astype(bf16)


def gate_grads_body(half, far_acts_ref, acts_ref, recv_ref, out_ref):
    sources, rows, total_wide = recv_ref.shape
    tok = acts_ref.shape[0]
    units = acts_ref.shape[1] // 4
    level, _ = level_and_side(half)
    ids, _ = read_meta(far_acts_ref)
    upper = (ids >= half).astype(f32)
    bin_of = (ids - half * upper) * 2 + jnp.abs(upper - level.astype(f32))
    chosen = slot_choice(bin_of, 2 * sources, rows // 2).astype(f32).astype(bf16)
    table = recv_ref[:, :, total_wide - units :].reshape(sources * rows, units)
    for choice in range(2):
        at = 2 * choice * units
        gate = acts_ref[:, at : at + units].astype(f32)
        up = acts_ref[:, at + units : at + 2 * units].astype(f32)
        grad = lax.dot_general(
            chosen[:, choice * tok : (choice + 1) * tok],
            table,
            (((0,), (0,)), ((), ())),
            preferred_element_type=f32,
        )
        sigmoid = jax.nn.sigmoid(gate)
        out_ref[:, at : at + units] = (
            grad * up * sigmoid * (1.0 + gate * (1.0 - sigmoid))
        ).astype(bf16)
        out_ref[:, at + units : at + 2 * units] = (grad * (gate * sigmoid)).astype(bf16)


def route_steps_body(source_ref, line_ref, recv_ref, out_ref):
    count, each, wide = out_ref.shape
    for k in range(count):
        line = pl.multiple_of(line_ref[k] * each, each)
        out_ref[k] = recv_ref[source_ref[k], pl.ds(line, each), 0:wide]


def place_steps_body(recv_ref, out_ref):
    halves, sources, sides, each, wide = recv_ref.shape
    for half in range(halves):
        for source in range(sources):
            for side in range(sides):
                at = (side * halves + half) * wide
                out_ref[source * each : (source + 1) * each, at : at + wide] = recv_ref[
                    half, source, side
                ]


def after(x, *others):
    return lax.optimization_barrier((x, *others))[0]


def mirrored_local(
    swap_pairs,
    expert_ids,
    route_weights,
    gate_up,
    grad_out,
    down_weight,
    first_moment,
    second_moment,
):
    places = lax.axis_size("expert")
    half = places // 2
    level, side = level_and_side(half)
    tok, top = expert_ids.shape
    units = down_weight.shape[1]
    wide = grad_out.shape[1]
    narrow = wide // 2
    cap = 2 * tok * top // places
    each = units // half
    across = [(k, (k + half) % places) for k in range(places)]
    beside = [(0, 1), (1, 0)]
    diagonal = [
        (2 * k + a, 2 * ((k + half) % places) + 1 - a) for k in range(places) for a in range(2)
    ]
    groups = [list(range(half)), list(range(half, places))]

    def mirror(x):
        return lax.ppermute(x, "expert", across)

    def neighbour(x):
        return lax.ppermute(x, "hidden", beside)

    def exchange(x):
        return lax.all_to_all(
            x, "expert", split_axis=0, concat_axis=0, tiled=True, axis_index_groups=groups
        )

    def shaped(*shape, dtype=bf16):
        return jax.ShapeDtypeStruct(shape, dtype)

    grads_far = [mirror(grad_out[: tok // 2]), mirror(grad_out[tok // 2 :])]
    acts = gate_up.reshape(tok, 4 * units)
    hidden, noted = whole_call(
        prepare_body, (shaped(top * tok, units), shaped(top * tok + 16, units)), "prepare"
    )(acts, expert_ids, route_weights)
    noted_far = mirror(noted)
    hidden_beside = neighbour(hidden)
    hidden_diagonal = lax.ppermute(hidden, ("expert", "hidden"), diagonal)

    state = (down_weight[0], first_moment[0], second_moment[0])
    split = whole_call(split_body, shaped(1, units, wide), "split_state")
    weight_beside = neighbour(split(state[0]))
    first_beside = neighbour(split(after(state[1], hidden)))
    second_beside = neighbour(split(after(state[2], hidden)))

    row = wide + 2 * units
    pack = functools.partial(
        whole_call, functools.partial(pack_body, half), shaped(half, cap, row)
    )
    packed = pack("pack_own")(noted, hidden_beside, grad_out)
    recv = exchange(after(packed, grads_far[0], weight_beside))
    packed_far = pack("pack_far")(noted_far, hidden_diagonal, *grads_far)
    recv_far = exchange(after(packed_far, recv, first_beside))
    recv_far = after(recv_far, second_beside)

    outputs = whole_call(forward_body, shaped(half, 2, cap, wide), "forward")(
        recv, recv_far, state[0], weight_beside
    )
    back = exchange(outputs.reshape(half, 2 * cap, wide)).reshape(half, 2, cap, wide)

    grad_keep, grad_send = whole_call(
        grad_hidden_body,
        (shaped(2, half, cap, units, dtype=f32), shaped(2, half, cap, units)),
        "grad_hidden",
    )(recv, recv_far, state[0], weight_beside)
    step, step_send = whole_call(
        functools.partial(update_body, half),
        (shaped(2, units, narrow), shaped(2, units, narrow)),
        "update",
    )(recv, recv_far, *state[1:], first_beside, second_beside)
    step_far = mirror(step_send)
    rows_own, rows_send = whole_call(
        add_sides_body, (shaped(half, cap, units), shaped(half, cap, units)), "add_sides"
    )(grad_keep, neighbour(grad_send))
    rows_far = mirror(rows_send)
    stacked = whole_call(stack_body, shaped(half, 2 * cap, narrow + units), "stack_steps")(
        step, step_far, rows_own, rows_far
    )
    combined_own, combined_send = whole_call(
        functools.partial(combine_body, half),
        (shaped(tok, wide, dtype=f32), shaped(tok, wide)),
        "combine",
    )(noted, noted_far, back)
    combined_far = mirror(combined_send)
    combined = whole_call(add_halves_body, shaped(tok, wide), "add_halves")(
        combined_own, combined_far
    )

    spread = exchange(after(stacked, back))

    partner = partner_table(swap_pairs, places)
    from_source = jnp.repeat(partner % half, 2)
    sides = jnp.tile(jnp.arange(2, dtype=jnp.int32), places)
    from_line = jnp.repeat((partner // half) ^ level, 2) * 2 + (sides ^ side)
    smem = pl.BlockSpec(memory_space=pltpu.SMEM)
    vmem = pl.BlockSpec(memory_space=pltpu.VMEM)
    routed = pl.pallas_call(
        route_steps_body,
        in_specs=[smem, smem, vmem],
        out_specs=vmem,
        out_shape=shaped(2 * places, each, narrow),
        name="route_steps",
        compiler_params=KERNEL_PARAMS,
    )(from_source.astype(jnp.int32), from_line.astype(jnp.int32), spread)
    placed = lax.all_to_all(
        after(routed, combined_far), ("expert", "hidden"), split_axis=0, concat_axis=0, tiled=True
    )

    grad_gate_up = whole_call(
        functools.partial(gate_grads_body, half), shaped(tok, 4 * units), "gate_grads"
    )(noted, acts, spread).reshape(gate_up.shape)
    adam_step = whole_call(place_steps_body, shaped(units, 2 * wide), "place_steps")(
        placed.reshape(2, half, 2, each, narrow)
    )
    return combined, grad_gate_up, adam_step[None]


def chosen_local(places, sides, *arrays):
    tok, top = arrays[1].shape
    units = arrays[5].shape[1]
    wide = arrays[4].shape[1]
    cap = 2 * tok * top // places
    fits = sides == 2 and top == 2 and places % 4 == 0 and places <= 256
    fits = fits and places * cap == 2 * tok * top and cap % 16 == 0
    fits = fits and wide % 256 == 0 and units == tok and tok % 128 == 0
    fits = fits and units % (8 * places) == 0 and 2 * cap == 4 * (units // (places // 2))
    return mirrored_local(*arrays) if fits else general_local(*arrays)


def solution(mesh):
    placed = (
        P(),
        P("expert", None),
        P("expert", None),
        P("expert", None, None, "hidden"),
        P("expert", "hidden"),
        P("expert", "hidden", None),
        P("expert", "hidden", None),
        P("expert", "hidden", None),
    )
    return jax.shard_map(
        functools.partial(chosen_local, mesh.shape["expert"], mesh.shape["hidden"]),
        mesh=mesh,
        in_specs=placed,
        out_specs=(
            P("expert", "hidden"),
            P("expert", None, None, "hidden"),
            P("expert", "hidden", None),
        ),
        check_vma=False,
    )
```

```python
import functools
import jax
import jax.numpy as jnp
from jax import lax
from jax.experimental import pallas as pl
from jax.experimental.pallas import tpu as pltpu
from jax.sharding import PartitionSpec as P

first_decay = 0.9
second_decay = 0.95
adam_epsilon = 1e-08


def partner_table(swap_pairs, places):
    column = jnp.arange(places, dtype=jnp.int32)
    left = swap_pairs[:, 0]
    right = swap_pairs[:, 1]
    moved = jnp.where(left[:, None] == column[None, :], right[:, None] - column[None, :], 0)
    moved = moved + jnp.where(right[:, None] == column[None, :], left[:, None] - column[None, :], 0)
    return column + jnp.sum(moved, axis=0)


def relocate_state(weight_here, first_here, second_here, partner):
    places = partner.shape[0]
    shape_here = weight_here.shape
    spread = (
        lax.all_to_all(
            weight_here.reshape(places, -1), "expert", split_axis=0, concat_axis=0, tiled=True
        ),
        lax.all_to_all(
            first_here.reshape(places, -1), "expert", split_axis=0, concat_axis=0, tiled=True
        ),
        lax.all_to_all(
            second_here.reshape(places, -1), "expert", split_axis=0, concat_axis=0, tiled=True
        ),
    )
    ordered = tuple((jnp.take(member, partner, axis=0) for member in spread))
    collected = (
        lax.all_to_all(ordered[0], "expert", split_axis=0, concat_axis=0, tiled=True),
        lax.all_to_all(ordered[1], "expert", split_axis=0, concat_axis=0, tiled=True),
        lax.all_to_all(ordered[2], "expert", split_axis=0, concat_axis=0, tiled=True),
    )
    return tuple((member.reshape(shape_here) for member in collected))


def slot_numbers(destination, places, capacity):
    column = jnp.arange(places, dtype=jnp.int32)
    one_hot = (destination[:, None] == column[None, :]).astype(jnp.int32)
    before = jnp.cumsum(one_hot, axis=0) - one_hot
    earlier_count = jnp.sum(before * one_hot, axis=1)
    return destination * capacity + earlier_count


def general_local(
    swap_pairs,
    expert_ids,
    route_weights,
    gate_up,
    grad_out,
    down_weight,
    first_moment,
    second_moment,
):
    places = lax.axis_size("expert")
    tok_count, top_count = expert_ids.shape
    hid_dev = down_weight.shape[1]
    capacity = 2 * tok_count * top_count // places
    total_slots = places * capacity
    choice_count = tok_count * top_count
    partner = partner_table(swap_pairs, places)
    weight_here = down_weight[0]
    first_here = first_moment[0]
    second_here = second_moment[0]
    flat_ids = expert_ids.reshape(-1)
    column = jnp.arange(places, dtype=jnp.int32)
    weight_here, first_here, second_here = relocate_state(
        weight_here, first_here, second_here, partner
    )
    destination = jnp.sum(
        jnp.where(flat_ids[:, None] == column[None, :], partner[None, :], 0), axis=1
    )
    slot_index = slot_numbers(destination, places, capacity)
    choice_acts = gate_up.reshape(choice_count, 2 * hid_dev)
    scaled = (route_weights[:, :, None] * grad_out[:, None, :].astype(jnp.float32)).astype(
        jnp.bfloat16
    )
    scaled = scaled.reshape(choice_count, grad_out.shape[1])
    send_acts = jnp.zeros((total_slots, 2 * hid_dev), jnp.bfloat16).at[slot_index].set(choice_acts)
    send_grads = (
        jnp.zeros((total_slots, grad_out.shape[1]), jnp.bfloat16).at[slot_index].set(scaled)
    )
    recv_acts, recv_grads = (
        lax.all_to_all(
            send_acts.reshape(places, capacity, 2 * hid_dev),
            "expert",
            split_axis=0,
            concat_axis=0,
            tiled=True,
        ),
        lax.all_to_all(
            send_grads.reshape(places, capacity, grad_out.shape[1]),
            "expert",
            split_axis=0,
            concat_axis=0,
            tiled=True,
        ),
    )
    recv_acts = recv_acts.reshape(total_slots, 2 * hid_dev)
    recv_grads = recv_grads.reshape(total_slots, grad_out.shape[1])
    gate_pre = recv_acts[:, :hid_dev].astype(jnp.float32)
    up_pre = recv_acts[:, hid_dev:].astype(jnp.float32)
    sigmoid_gate = jax.nn.sigmoid(gate_pre)
    silu_gate = gate_pre * sigmoid_gate
    hidden = (silu_gate * up_pre).astype(jnp.bfloat16)
    partial_value = jnp.dot(hidden, weight_here, preferred_element_type=jnp.float32)
    summed = lax.psum_scatter(
        partial_value.astype(jnp.bfloat16), "hidden", scatter_dimension=1, tiled=True
    ).astype(jnp.float32)
    returned = lax.all_to_all(
        summed.reshape(places, capacity, summed.shape[1]).astype(jnp.bfloat16),
        "expert",
        split_axis=0,
        concat_axis=0,
        tiled=True,
    ).astype(jnp.float32)
    per_choice = jnp.take(returned.reshape(total_slots, summed.shape[1]), slot_index, axis=0)
    per_choice = per_choice.reshape(tok_count, top_count, summed.shape[1])
    combined = jnp.einsum("tk,tkd->td", route_weights, per_choice).astype(jnp.bfloat16)
    portion = lax.all_gather(recv_grads, "hidden", axis=1, tiled=True)
    grad_hidden = lax.dot_general(
        portion, weight_here, (((1,), (1,)), ((), ())), preferred_element_type=jnp.float32
    )
    product_block = lax.dot_general(
        hidden, portion, (((0,), (0,)), ((), ())), preferred_element_type=jnp.float32
    )
    grad_weight = product_block
    grad_hidden, grad_weight = (grad_hidden, grad_weight)
    grad_gate = grad_hidden * up_pre * sigmoid_gate * (1.0 + gate_pre * (1.0 - sigmoid_gate))
    grad_up = grad_hidden * silu_gate
    grad_rows = jnp.concatenate([grad_gate, grad_up], axis=1).astype(jnp.bfloat16)
    returned_grads = lax.all_to_all(
        grad_rows.reshape(places, capacity, 2 * hid_dev),
        "expert",
        split_axis=0,
        concat_axis=0,
        tiled=True,
    )
    grad_gate_up = jnp.take(returned_grads.reshape(total_slots, 2 * hid_dev), slot_index, axis=0)
    grad_gate_up = grad_gate_up.reshape(tok_count, top_count, 2, hid_dev)
    first_new = first_decay * first_here.astype(jnp.float32) + (1.0 - first_decay) * grad_weight
    second_new = (
        second_decay * second_here.astype(jnp.float32)
        + (1.0 - second_decay) * grad_weight * grad_weight
    )
    update = (first_new / (jnp.sqrt(second_new) + adam_epsilon)).astype(jnp.bfloat16)
    return (combined, grad_gate_up, update[None])


bf16 = jnp.bfloat16
f32 = jnp.float32
HEAVY = 10_000_000_000
KERNEL_PARAMS = pltpu.CompilerParams(vmem_limit_bytes=40 * 1024 * 1024)


def whole_call(body, out_shape, name, moved=None):
    cost = None if moved is None else pl.CostEstimate(flops=100 * moved, bytes_accessed=moved, transcendentals=0)
    return pl.pallas_call(
        body, out_shape=out_shape, name=name, compiler_params=KERNEL_PARAMS, cost_estimate=cost
    )


def level_and_side(half):
    return lax.axis_index("expert") // half, lax.axis_index("hidden")


def columns_at(ref, index, wide):
    return ref[:, pl.ds(pl.multiple_of(index * wide, wide), wide)]


def same_index(size):
    first = lax.broadcasted_iota(jnp.int32, (size, size), 0)
    second = lax.broadcasted_iota(jnp.int32, (size, size), 1)
    return first == second


def prepare_body(acts_ref, ids_ref, weights_ref, hidden_ref, far_ref):
    tok = acts_ref.shape[0]
    units = acts_ref.shape[1] // 4
    for choice in range(2):
        at = 2 * choice * units
        gate = acts_ref[:, at : at + units].astype(f32)
        up = acts_ref[:, at + units : at + 2 * units].astype(f32)
        value = (gate * jax.nn.sigmoid(gate) * up).astype(bf16)
        hidden_ref[choice * tok : (choice + 1) * tok, :] = value
        far_ref[choice * tok : (choice + 1) * tok, :] = value
    weights = weights_ref[...]
    high = weights.astype(bf16)
    middle = (weights - high.astype(f32)).astype(bf16)
    low = (weights - high.astype(f32) - middle.astype(f32)).astype(bf16)
    unit = same_index(tok).astype(f32).astype(bf16)
    pieces = [
        lax.dot_general(piece, unit, (((0,), (0,)), ((), ())), preferred_element_type=f32)
        for piece in (ids_ref[...].astype(f32).astype(bf16), high, middle, low)
    ]
    blank = jnp.zeros((16 - 8, tok), f32)
    far_ref[2 * tok : 2 * tok + 16, :] = jnp.concatenate(pieces + [blank], axis=0).astype(bf16)


def split_body(*refs):
    out_ref = refs[-1]
    side = lax.axis_index("hidden")
    for k, ref in enumerate(refs[:-1]):
        out_ref[k] = columns_at(ref, 1 - side, ref.shape[1] // 2)


def read_meta(ref):
    tok = ref.shape[1]
    meta = ref[2 * tok : 2 * tok + 16, :].astype(f32)
    ids = jnp.concatenate([meta[0:1, :], meta[1:2, :]], axis=1)
    weights = [
        meta[2 + k : 3 + k, :] + meta[4 + k : 5 + k, :] + meta[6 + k : 7 + k, :] for k in range(2)
    ]
    return ids, weights


def slot_choice(bin_of, bins, cap):
    count = bin_of.shape[1]
    column = lax.broadcasted_iota(jnp.int32, (bins, count), 0).astype(f32)
    one_hot = (bin_of == column).astype(f32)
    first = lax.broadcasted_iota(jnp.int32, (count, count), 0)
    second = lax.broadcasted_iota(jnp.int32, (count, count), 1)
    earlier = (first < second).astype(f32).astype(bf16)
    rank = jnp.dot(one_hot.astype(bf16), earlier, preferred_element_type=f32)
    slot = jnp.sum(one_hot * (rank + column * cap + 1.0), axis=0, keepdims=True) - 1.0
    return slot == lax.broadcasted_iota(jnp.int32, (bins * cap, count), 0).astype(f32)


def pack_body(half, acts_ref, beside_ref, *refs):
    out_ref = refs[-1]
    bins, cap, _ = out_ref.shape
    units = beside_ref.shape[1]
    grads = jnp.concatenate([ref[...] for ref in refs[:-1]], axis=0)
    tok, wide = grads.shape
    level, _ = level_and_side(half)
    ids, weights = read_meta(acts_ref)
    chosen = slot_choice(ids - (half * level).astype(f32), bins, cap)
    weights = jnp.concatenate(weights, axis=1)
    factor = jnp.sum(jnp.where(chosen, weights, 0.0), axis=1, keepdims=True)
    one_hot = chosen.astype(f32)
    by_token = (one_hot[:, :tok] + one_hot[:, tok:]).astype(bf16)
    rows = jnp.dot(by_token, grads, preferred_element_type=f32)
    out_ref[:, :, 0:wide] = (rows * factor).astype(bf16).reshape(bins, cap, wide)
    for side, ref in enumerate((acts_ref, beside_ref)):
        at = wide + side * units
        acts = jnp.dot(
            one_hot.astype(bf16), ref[0 : 2 * tok, :], preferred_element_type=f32
        )
        out_ref[:, :, at : at + units] = acts.astype(bf16).reshape(bins, cap, units)


def rows_of(ref, start, size):
    sources, cap, _ = ref.shape
    return ref[:, :, start : start + size].reshape(sources * cap, size)


def place_in_half(half):
    return lax.rem(lax.axis_index("expert"), half)


def forward_body(half, block, recv_ref, weight_ref, beside_ref, *out_refs):
    cap, wide = out_refs[0].shape[-2:]
    units = weight_ref.shape[0]
    me = place_in_half(half)
    acts = jnp.concatenate([recv_ref[me ^ r, :, wide:] for r in range(half)], axis=0)
    total = jnp.dot(
        acts[:, :units],
        columns_at(weight_ref, lax.axis_index("hidden"), wide),
        preferred_element_type=f32,
    )
    total = total + jnp.dot(acts[:, units:], beside_ref[0], preferred_element_type=f32)
    total = total.astype(bf16).reshape(half // 2, 2, cap, wide)
    if block == 1:
        for distance, ref in enumerate(out_refs):
            ref[...] = total[distance]
    else:
        for core, ref in enumerate(out_refs):
            ref[...] = total[:, core]


def join_cores_body(keep_ref, got_ref, *out_refs):
    for distance, ref in enumerate(out_refs):
        ref[0] = keep_ref[distance]
        ref[1] = got_ref[distance]


def other_core_body(*refs):
    out_ref = refs[-1]
    for distance, ref in enumerate(refs[:-1]):
        out_ref[distance] = ref[1]


def update_body(
    half,
    recv_ref,
    far_ref,
    weight_ref,
    first_ref,
    second_ref,
    weight_beside,
    first_beside,
    second_beside,
    out_ref,
):
    _, units, wide = first_beside.shape
    level, here = level_and_side(half)
    groups = out_ref.shape[0]
    narrow = wide // 2
    each = units // groups
    acts = jnp.concatenate([rows_of(ref, wide, 2 * units) for ref in (recv_ref, far_ref)], axis=0)
    scaled = jnp.concatenate([rows_of(ref, 0, wide) for ref in (recv_ref, far_ref)], axis=0)
    for part in range(2):
        grads = lax.dot_general(
            acts,
            scaled[:, part * narrow : (part + 1) * narrow],
            (((0,), (0,)), ((), ())),
            preferred_element_type=f32,
        )
        for side in range(2):
            if side == 0:
                moments = [
                    columns_at(ref, 2 * here + part, narrow) for ref in (first_ref, second_ref)
                ]
            else:
                moments = [
                    ref[0, :, part * narrow : (part + 1) * narrow]
                    for ref in (first_beside, second_beside)
                ]
            grad = grads[side * units : (side + 1) * units]
            first = first_decay * moments[0].astype(f32) + (1.0 - first_decay) * grad
            second = second_decay * moments[1].astype(f32)
            second = second + (1.0 - second_decay) * grad * grad
            step = (first / (jnp.sqrt(second) + adam_epsilon)).astype(bf16)
            out_ref[:, part, side * each : (side + 1) * each, 0:narrow] = step.reshape(
                groups, each, narrow
            )
    own = columns_at(weight_ref, here, wide)
    for part, weight in enumerate((own, weight_beside[0])):
        rows = lax.dot_general(
            scaled, weight, (((1,), (1,)), ((), ())), preferred_element_type=f32
        ).astype(bf16)
        rows = rows.reshape(2, half // 2, 2, -1, units)
        at = narrow + part * units
        for block, place in enumerate((level, 1 - level)):
            lines = pl.ds(place * (half // 2), half // 2)
            for odd in range(2):
                out_ref[lines, odd, :, at : at + units] = rows[block, :, odd]


def combine_far_body(half, acts_ref, *refs):
    near_refs, other_ref, out_ref = refs[:-2], refs[-2], refs[-1]
    pieces = []
    for distance, ref in enumerate(near_refs):
        pieces += [ref[0], other_ref[distance]]
    out_ref[...] = combined(half, acts_ref, pieces, out_ref.shape[0]).astype(bf16)


def combine_own_body(half, acts_ref, far_ref, *refs):
    out_ref = refs[-1]
    pieces = [ref[core] for ref in refs[:-1] for core in range(2)]
    total = combined(half, acts_ref, pieces, out_ref.shape[0])
    out_ref[...] = (total + far_ref[...].astype(f32)).astype(bf16)


def combined(half, acts_ref, pieces, tok):
    cap = pieces[0].shape[0]
    level, _ = level_and_side(half)
    diagonal = same_index(tok)
    ids, weights = read_meta(acts_ref)
    ids = ids.astype(jnp.int32) - half * level
    inside = (ids >= 0) & (ids < half)
    bin_of = jnp.where(inside, ids ^ place_in_half(half), -1).astype(f32)
    chosen = slot_choice(bin_of, half, cap).astype(f32).astype(bf16)
    rows = jnp.concatenate(pieces, axis=0)
    total = None
    for choice in range(2):
        picked = lax.dot_general(
            chosen[:, choice * tok : (choice + 1) * tok],
            rows,
            (((0,), (0,)), ((), ())),
            preferred_element_type=f32,
        )
        upright = jnp.sum(jnp.where(diagonal, weights[choice], 0.0), axis=1, keepdims=True)
        part = upright * picked
        total = part if total is None else total + part
    return total


def pick_grads_body(meta_ref, recv_ref, own_ref, send_ref):
    places, rows, total_wide = recv_ref.shape
    units = own_ref.shape[1]
    ids, _ = read_meta(meta_ref)
    chosen = slot_choice(ids, places, rows).astype(f32).astype(bf16)
    for part, out_ref in enumerate((own_ref, send_ref)):
        at = total_wide - (2 - part) * units
        picked = lax.dot_general(
            chosen,
            recv_ref[:, :, at : at + units].reshape(places * rows, units),
            (((0,), (0,)), ((), ())),
            preferred_element_type=f32,
        )
        out_ref[...] = picked.astype(out_ref.dtype)


def gate_grads_body(acts_ref, own_ref, got_ref, out_ref):
    tok = acts_ref.shape[0]
    units = own_ref.shape[1]
    for choice in range(2):
        at = 2 * choice * units
        lines = slice(choice * tok, (choice + 1) * tok)
        gate = acts_ref[:, at : at + units].astype(f32)
        up = acts_ref[:, at + units : at + 2 * units].astype(f32)
        grad = own_ref[lines, :] + got_ref[lines, :].astype(f32)
        sigmoid = jax.nn.sigmoid(gate)
        out_ref[:, at : at + units] = (
            grad * up * sigmoid * (1.0 + gate * (1.0 - sigmoid))
        ).astype(bf16)
        out_ref[:, at + units : at + 2 * units] = (grad * (gate * sigmoid)).astype(bf16)


def route_steps_body(source_ref, line_ref, recv_ref, out_ref):
    count, each, wide = out_ref.shape
    for k in range(count):
        line = pl.multiple_of(line_ref[k] * each, each)
        out_ref[k] = recv_ref[source_ref[k], pl.ds(line, each), 0:wide]


def place_steps_body(recv_ref, out_ref):
    groups, parts, sides, each, wide = recv_ref.shape
    for group in range(groups):
        for part in range(parts):
            for side in range(sides):
                at = (side * parts + part) * wide
                out_ref[group * each : (group + 1) * each, at : at + wide] = recv_ref[
                    group, part, side
                ]


def after(x, *others):
    return lax.optimization_barrier((x, *others))[0]


def mirrored_local(
    swap_pairs,
    expert_ids,
    route_weights,
    gate_up,
    grad_out,
    down_weight,
    first_moment,
    second_moment,
):
    places = lax.axis_size("expert")
    half = places // 2
    level, side = level_and_side(half)
    tok, top = expert_ids.shape
    units = down_weight.shape[1]
    wide = grad_out.shape[1]
    narrow = wide // 2
    cap = 2 * tok * top // places
    each = units // half
    across = [(k, (k + half) % places) for k in range(places)]
    beside = [(0, 1), (1, 0)]
    diagonal = [
        (2 * k + a, 2 * ((k + half) % places) + 1 - a) for k in range(places) for a in range(2)
    ]
    groups = [list(range(half)), list(range(half, places))]

    def mirror(x):
        return lax.ppermute(x, "expert", across)

    def neighbour(x):
        return lax.ppermute(x, "hidden", beside)

    def exchange(x):
        return lax.all_to_all(
            x, "expert", split_axis=0, concat_axis=0, tiled=True, axis_index_groups=groups
        )

    def shaped(*shape, dtype=bf16):
        return jax.ShapeDtypeStruct(shape, dtype)

    grads_far = [mirror(grad_out)]
    acts = gate_up.reshape(tok, 4 * units)
    hidden, noted = whole_call(
        prepare_body, (shaped(top * tok, units), shaped(top * tok + 16, units)), "prepare"
    )(acts, expert_ids, route_weights)
    noted_far = mirror(noted)
    hidden_beside = neighbour(hidden)
    hidden_diagonal = lax.ppermute(hidden, ("expert", "hidden"), diagonal)

    state = (down_weight[0], first_moment[0], second_moment[0])
    split = whole_call(split_body, shaped(1, units, wide), "split_state")
    weight_beside = neighbour(split(state[0]))
    first_beside = neighbour(split(after(state[1], hidden)))
    second_beside = neighbour(split(after(state[2], hidden)))

    row = wide + 2 * units
    pack = functools.partial(
        whole_call, functools.partial(pack_body, half), shaped(half, cap, row)
    )
    packed = pack("pack_own")(noted, hidden_beside, grad_out)
    recv = exchange(packed)

    packed_far = pack("pack_far", moved=HEAVY)(noted_far, hidden_diagonal, *grads_far)
    recv, packed_far, weight_beside, first_beside = lax.optimization_barrier(
        (recv, packed_far, weight_beside, first_beside)
    )
    recv_far = exchange(packed_far)
    recv_far, second_beside = lax.optimization_barrier((recv_far, second_beside))

    def forward(rows, block, shape, name):
        return whole_call(functools.partial(forward_body, half, block), shape, name)(
            rows, state[0], weight_beside
        )

    def at_distance(x, distance):
        return lax.ppermute(x, "expert", [(k, k ^ distance) for k in range(places)])

    def by_chip(outputs):
        return [outputs[0]] + [at_distance(outputs[k], 2 * k) for k in range(1, half // 2)]

    pairs = (shaped(2, cap, wide),) * (half // 2)
    cores = (shaped(half // 2, cap, wide),) * 2

    outputs_far = forward(recv_far, 1, pairs, "forward_far")
    steps = whole_call(
        functools.partial(update_body, half),
        shaped(half, 2, 2 * each, narrow + 2 * units),
        "update",
    )(recv, after(recv_far, outputs_far), *state, weight_beside, first_beside, second_beside)
    spread = lax.all_to_all(
        steps.reshape(places, 2 * each, narrow + 2 * units),
        "expert",
        split_axis=0,
        concat_axis=0,
        tiled=True,
    )

    near_far = by_chip(outputs_far)
    near_far, steps = lax.optimization_barrier((near_far, steps))
    crossing = whole_call(other_core_body, cores[0], "other_core_far")(*near_far)
    combined_send = whole_call(
        functools.partial(combine_far_body, half), shaped(tok, wide), "combine_far", HEAVY
    )(noted_far, *near_far, at_distance(crossing, 1))
    combined_far = mirror(combined_send)
    keep_core, send_core = forward(after(recv, combined_send), 0, cores, "forward_own")
    joined = whole_call(join_cores_body, pairs, "join_cores")(
        keep_core, at_distance(send_core, 1)
    )
    near = by_chip(joined)

    partner = partner_table(swap_pairs, places)
    sides = jnp.tile(jnp.arange(2, dtype=jnp.int32), places)
    smem = pl.BlockSpec(memory_space=pltpu.SMEM)
    vmem = pl.BlockSpec(memory_space=pltpu.VMEM)
    routed = pl.pallas_call(
        route_steps_body,
        in_specs=[smem, smem, vmem],
        out_specs=vmem,
        out_shape=shaped(2 * places, each, narrow),
        name="route_steps",
        compiler_params=KERNEL_PARAMS,
    )(jnp.repeat(partner, 2).astype(jnp.int32), (sides ^ side).astype(jnp.int32), spread)
    placed = lax.all_to_all(
        after(routed, combined_send), ("expert", "hidden"), split_axis=0, concat_axis=0, tiled=True
    )

    rows_own, rows_send = whole_call(
        pick_grads_body,
        (shaped(top * tok, units, dtype=f32), shaped(top * tok, units)),
        "pick_grads",
        HEAVY,
    )(noted, spread)
    grad_gate_up = whole_call(gate_grads_body, shaped(tok, 4 * units), "gate_grads")(
        acts, rows_own, neighbour(rows_send)
    ).reshape(gate_up.shape)

    near, combined_far = lax.optimization_barrier((near, combined_far, rows_own))[:2]
    combined = whole_call(
        functools.partial(combine_own_body, half), shaped(tok, wide), "combine_own"
    )(noted, combined_far, *near)
    adam_step = whole_call(place_steps_body, shaped(units, 2 * wide), "place_steps")(
        placed.reshape(half, 2, 2, each, narrow)
    )
    return combined, grad_gate_up, adam_step[None]


def chosen_local(places, sides, *arrays):
    tok, top = arrays[1].shape
    units = arrays[5].shape[1]
    wide = arrays[4].shape[1]
    cap = 2 * tok * top // places
    fits = sides == 2 and top == 2 and places % 4 == 0 and places <= 256
    fits = fits and places * cap == 2 * tok * top and cap % 16 == 0
    fits = fits and wide % 256 == 0 and units == tok and tok % 128 == 0
    fits = fits and places & (places - 1) == 0 and (units // (places // 2)) % 16 == 0
    fits = fits and cap == 2 * (units // (places // 2))
    return mirrored_local(*arrays) if fits else general_local(*arrays)


def solution(mesh):
    placed = (
        P(),
        P("expert", None),
        P("expert", None),
        P("expert", None, None, "hidden"),
        P("expert", "hidden"),
        P("expert", "hidden", None),
        P("expert", "hidden", None),
        P("expert", "hidden", None),
    )
    return jax.shard_map(
        functools.partial(chosen_local, mesh.shape["expert"], mesh.shape["hidden"]),
        mesh=mesh,
        in_specs=placed,
        out_specs=(
            P("expert", "hidden"),
            P("expert", None, None, "hidden"),
            P("expert", "hidden", None),
        ),
        check_vma=False,
    )
```

```python
import functools
import jax
import jax.numpy as jnp
from jax import lax
from jax.experimental import pallas as pl
from jax.experimental.pallas import tpu as pltpu
from jax.sharding import PartitionSpec as P

first_decay = 0.9
second_decay = 0.95
adam_epsilon = 1e-08


def partner_table(swap_pairs, places):
    column = jnp.arange(places, dtype=jnp.int32)
    left = swap_pairs[:, 0]
    right = swap_pairs[:, 1]
    moved = jnp.where(left[:, None] == column[None, :], right[:, None] - column[None, :], 0)
    moved = moved + jnp.where(right[:, None] == column[None, :], left[:, None] - column[None, :], 0)
    return column + jnp.sum(moved, axis=0)


def relocate_state(weight_here, first_here, second_here, partner):
    places = partner.shape[0]
    shape_here = weight_here.shape
    spread = (
        lax.all_to_all(
            weight_here.reshape(places, -1), "expert", split_axis=0, concat_axis=0, tiled=True
        ),
        lax.all_to_all(
            first_here.reshape(places, -1), "expert", split_axis=0, concat_axis=0, tiled=True
        ),
        lax.all_to_all(
            second_here.reshape(places, -1), "expert", split_axis=0, concat_axis=0, tiled=True
        ),
    )
    ordered = tuple((jnp.take(member, partner, axis=0) for member in spread))
    collected = (
        lax.all_to_all(ordered[0], "expert", split_axis=0, concat_axis=0, tiled=True),
        lax.all_to_all(ordered[1], "expert", split_axis=0, concat_axis=0, tiled=True),
        lax.all_to_all(ordered[2], "expert", split_axis=0, concat_axis=0, tiled=True),
    )
    return tuple((member.reshape(shape_here) for member in collected))


def slot_numbers(destination, places, capacity):
    column = jnp.arange(places, dtype=jnp.int32)
    one_hot = (destination[:, None] == column[None, :]).astype(jnp.int32)
    before = jnp.cumsum(one_hot, axis=0) - one_hot
    earlier_count = jnp.sum(before * one_hot, axis=1)
    return destination * capacity + earlier_count


def general_local(
    swap_pairs,
    expert_ids,
    route_weights,
    gate_up,
    grad_out,
    down_weight,
    first_moment,
    second_moment,
):
    places = lax.axis_size("expert")
    tok_count, top_count = expert_ids.shape
    hid_dev = down_weight.shape[1]
    capacity = 2 * tok_count * top_count // places
    total_slots = places * capacity
    choice_count = tok_count * top_count
    partner = partner_table(swap_pairs, places)
    weight_here = down_weight[0]
    first_here = first_moment[0]
    second_here = second_moment[0]
    flat_ids = expert_ids.reshape(-1)
    column = jnp.arange(places, dtype=jnp.int32)
    weight_here, first_here, second_here = relocate_state(
        weight_here, first_here, second_here, partner
    )
    destination = jnp.sum(
        jnp.where(flat_ids[:, None] == column[None, :], partner[None, :], 0), axis=1
    )
    slot_index = slot_numbers(destination, places, capacity)
    choice_acts = gate_up.reshape(choice_count, 2 * hid_dev)
    scaled = (route_weights[:, :, None] * grad_out[:, None, :].astype(jnp.float32)).astype(
        jnp.bfloat16
    )
    scaled = scaled.reshape(choice_count, grad_out.shape[1])
    send_acts = jnp.zeros((total_slots, 2 * hid_dev), jnp.bfloat16).at[slot_index].set(choice_acts)
    send_grads = (
        jnp.zeros((total_slots, grad_out.shape[1]), jnp.bfloat16).at[slot_index].set(scaled)
    )
    recv_acts, recv_grads = (
        lax.all_to_all(
            send_acts.reshape(places, capacity, 2 * hid_dev),
            "expert",
            split_axis=0,
            concat_axis=0,
            tiled=True,
        ),
        lax.all_to_all(
            send_grads.reshape(places, capacity, grad_out.shape[1]),
            "expert",
            split_axis=0,
            concat_axis=0,
            tiled=True,
        ),
    )
    recv_acts = recv_acts.reshape(total_slots, 2 * hid_dev)
    recv_grads = recv_grads.reshape(total_slots, grad_out.shape[1])
    gate_pre = recv_acts[:, :hid_dev].astype(jnp.float32)
    up_pre = recv_acts[:, hid_dev:].astype(jnp.float32)
    sigmoid_gate = jax.nn.sigmoid(gate_pre)
    silu_gate = gate_pre * sigmoid_gate
    hidden = (silu_gate * up_pre).astype(jnp.bfloat16)
    partial_value = jnp.dot(hidden, weight_here, preferred_element_type=jnp.float32)
    summed = lax.psum_scatter(
        partial_value.astype(jnp.bfloat16), "hidden", scatter_dimension=1, tiled=True
    ).astype(jnp.float32)
    returned = lax.all_to_all(
        summed.reshape(places, capacity, summed.shape[1]).astype(jnp.bfloat16),
        "expert",
        split_axis=0,
        concat_axis=0,
        tiled=True,
    ).astype(jnp.float32)
    per_choice = jnp.take(returned.reshape(total_slots, summed.shape[1]), slot_index, axis=0)
    per_choice = per_choice.reshape(tok_count, top_count, summed.shape[1])
    combined = jnp.einsum("tk,tkd->td", route_weights, per_choice).astype(jnp.bfloat16)
    portion = lax.all_gather(recv_grads, "hidden", axis=1, tiled=True)
    grad_hidden = lax.dot_general(
        portion, weight_here, (((1,), (1,)), ((), ())), preferred_element_type=jnp.float32
    )
    product_block = lax.dot_general(
        hidden, portion, (((0,), (0,)), ((), ())), preferred_element_type=jnp.float32
    )
    grad_weight = product_block
    grad_hidden, grad_weight = (grad_hidden, grad_weight)
    grad_gate = grad_hidden * up_pre * sigmoid_gate * (1.0 + gate_pre * (1.0 - sigmoid_gate))
    grad_up = grad_hidden * silu_gate
    grad_rows = jnp.concatenate([grad_gate, grad_up], axis=1).astype(jnp.bfloat16)
    returned_grads = lax.all_to_all(
        grad_rows.reshape(places, capacity, 2 * hid_dev),
        "expert",
        split_axis=0,
        concat_axis=0,
        tiled=True,
    )
    grad_gate_up = jnp.take(returned_grads.reshape(total_slots, 2 * hid_dev), slot_index, axis=0)
    grad_gate_up = grad_gate_up.reshape(tok_count, top_count, 2, hid_dev)
    first_new = first_decay * first_here.astype(jnp.float32) + (1.0 - first_decay) * grad_weight
    second_new = (
        second_decay * second_here.astype(jnp.float32)
        + (1.0 - second_decay) * grad_weight * grad_weight
    )
    update = (first_new / (jnp.sqrt(second_new) + adam_epsilon)).astype(jnp.bfloat16)
    return (combined, grad_gate_up, update[None])


bf16 = jnp.bfloat16
f32 = jnp.float32
HEAVY = 10_000_000_000
KERNEL_PARAMS = pltpu.CompilerParams(vmem_limit_bytes=40 * 1024 * 1024)


def whole_call(body, out_shape, name, moved=None):
    cost = None if moved is None else pl.CostEstimate(flops=100 * moved, bytes_accessed=moved, transcendentals=0)
    return pl.pallas_call(
        body, out_shape=out_shape, name=name, compiler_params=KERNEL_PARAMS, cost_estimate=cost
    )


def level_and_side(half):
    return lax.axis_index("expert") // half, lax.axis_index("hidden")


def columns_at(ref, index, wide):
    return ref[:, pl.ds(pl.multiple_of(index * wide, wide), wide)]


def same_index(size):
    first = lax.broadcasted_iota(jnp.int32, (size, size), 0)
    second = lax.broadcasted_iota(jnp.int32, (size, size), 1)
    return first == second


def prepare_body(acts_ref, choices_ref, hidden_ref, far_ref):
    tok = acts_ref.shape[0]
    units = acts_ref.shape[1] // 4
    for choice in range(2):
        at = 2 * choice * units
        gate = acts_ref[:, at : at + units].astype(f32)
        up = acts_ref[:, at + units : at + 2 * units].astype(f32)
        value = (gate * jax.nn.sigmoid(gate) * up).astype(bf16)
        hidden_ref[choice * tok : (choice + 1) * tok, :] = value
        far_ref[choice * tok : (choice + 1) * tok, :] = value
    ids, weights = choices_ref[:, 0:2], choices_ref[:, 2:4]
    high = weights.astype(bf16)
    middle = (weights - high.astype(f32)).astype(bf16)
    low = (weights - high.astype(f32) - middle.astype(f32)).astype(bf16)
    unit = same_index(tok).astype(f32).astype(bf16)
    pieces = [
        lax.dot_general(piece, unit, (((0,), (0,)), ((), ())), preferred_element_type=f32)
        for piece in (ids.astype(bf16), high, middle, low)
    ]
    blank = jnp.zeros((16 - 8, tok), f32)
    far_ref[2 * tok : 2 * tok + 16, :] = jnp.concatenate(pieces + [blank], axis=0).astype(bf16)


def split_body(*refs):
    out_ref = refs[-1]
    side = lax.axis_index("hidden")
    for k, ref in enumerate(refs[:-1]):
        out_ref[k] = columns_at(ref, 1 - side, ref.shape[1] // 2)


def read_meta(ref):
    tok = ref.shape[1]
    meta = ref[2 * tok : 2 * tok + 16, :].astype(f32)
    ids = jnp.concatenate([meta[0:1, :], meta[1:2, :]], axis=1)
    weights = [
        meta[2 + k : 3 + k, :] + meta[4 + k : 5 + k, :] + meta[6 + k : 7 + k, :] for k in range(2)
    ]
    return ids, weights


def slot_choice(bin_of, bins, cap):
    count = bin_of.shape[1]
    column = lax.broadcasted_iota(jnp.int32, (bins, count), 0).astype(f32)
    one_hot = (bin_of == column).astype(f32)
    first = lax.broadcasted_iota(jnp.int32, (count, count), 0)
    second = lax.broadcasted_iota(jnp.int32, (count, count), 1)
    earlier = (first < second).astype(f32).astype(bf16)
    rank = jnp.dot(one_hot.astype(bf16), earlier, preferred_element_type=f32)
    slot = jnp.sum(one_hot * (rank + column * cap + 1.0), axis=0, keepdims=True) - 1.0
    return slot == lax.broadcasted_iota(jnp.int32, (bins * cap, count), 0).astype(f32)


def pack_body(half, acts_ref, beside_ref, *refs):
    out_ref = refs[-1]
    bins, cap, _ = out_ref.shape
    units = beside_ref.shape[1]
    grads = jnp.concatenate([ref[...] for ref in refs[:-1]], axis=0)
    tok, wide = grads.shape
    level, _ = level_and_side(half)
    ids, weights = read_meta(acts_ref)
    chosen = slot_choice(ids - (half * level).astype(f32), bins, cap)
    weights = jnp.concatenate(weights, axis=1)
    factor = jnp.sum(jnp.where(chosen, weights, 0.0), axis=1, keepdims=True)
    one_hot = chosen.astype(f32)
    by_token = (one_hot[:, :tok] + one_hot[:, tok:]).astype(bf16)
    rows = jnp.dot(by_token, grads, preferred_element_type=f32)
    out_ref[:, :, 0:wide] = (rows * factor).astype(bf16).reshape(bins, cap, wide)
    for side, ref in enumerate((acts_ref, beside_ref)):
        at = wide + side * units
        acts = jnp.dot(
            one_hot.astype(bf16), ref[0 : 2 * tok, :], preferred_element_type=f32
        )
        out_ref[:, :, at : at + units] = acts.astype(bf16).reshape(bins, cap, units)


def rows_of(ref, start, size):
    sources, cap, _ = ref.shape
    return ref[:, :, start : start + size].reshape(sources * cap, size)


def place_in_half(half):
    return lax.rem(lax.axis_index("expert"), half)


def forward_body(half, block, recv_ref, weight_ref, beside_ref, *out_refs):
    cap, wide = out_refs[0].shape[-2:]
    units = weight_ref.shape[0]
    me = place_in_half(half)
    acts = jnp.concatenate([recv_ref[me ^ r, :, wide:] for r in range(half)], axis=0)
    total = jnp.dot(
        acts[:, :units],
        columns_at(weight_ref, lax.axis_index("hidden"), wide),
        preferred_element_type=f32,
    )
    total = total + jnp.dot(acts[:, units:], beside_ref[0], preferred_element_type=f32)
    total = total.astype(bf16).reshape(half // 2, 2, cap, wide)
    if block == 1:
        for distance, ref in enumerate(out_refs):
            ref[...] = total[distance]
    else:
        for core, ref in enumerate(out_refs):
            ref[...] = total[:, core]


def join_cores_body(keep_ref, got_ref, *out_refs):
    for distance, ref in enumerate(out_refs):
        ref[0] = keep_ref[distance]
        ref[1] = got_ref[distance]


def other_core_body(*refs):
    out_ref = refs[-1]
    for distance, ref in enumerate(refs[:-1]):
        out_ref[distance] = ref[1]


def update_body(
    half,
    recv_ref,
    far_ref,
    weight_ref,
    first_ref,
    second_ref,
    weight_beside,
    first_beside,
    second_beside,
    out_ref,
):
    _, units, wide = first_beside.shape
    level, here = level_and_side(half)
    groups = out_ref.shape[0]
    narrow = wide // 2
    each = units // groups
    acts = jnp.concatenate([rows_of(ref, wide, 2 * units) for ref in (recv_ref, far_ref)], axis=0)
    scaled = jnp.concatenate([rows_of(ref, 0, wide) for ref in (recv_ref, far_ref)], axis=0)
    for part in range(2):
        grads = lax.dot_general(
            acts,
            scaled[:, part * narrow : (part + 1) * narrow],
            (((0,), (0,)), ((), ())),
            preferred_element_type=f32,
        )
        for side in range(2):
            if side == 0:
                moments = [
                    columns_at(ref, 2 * here + part, narrow) for ref in (first_ref, second_ref)
                ]
            else:
                moments = [
                    ref[0, :, part * narrow : (part + 1) * narrow]
                    for ref in (first_beside, second_beside)
                ]
            grad = grads[side * units : (side + 1) * units]
            first = first_decay * moments[0].astype(f32) + (1.0 - first_decay) * grad
            second = second_decay * moments[1].astype(f32)
            second = second + (1.0 - second_decay) * grad * grad
            root = second * lax.rsqrt(second) + adam_epsilon
            step = (first * pl.reciprocal(root, approx=True)).astype(bf16)
            out_ref[:, part, side * each : (side + 1) * each, 0:narrow] = step.reshape(
                groups, each, narrow
            )
    own = columns_at(weight_ref, here, wide)
    for part, weight in enumerate((own, weight_beside[0])):
        rows = lax.dot_general(
            scaled, weight, (((1,), (1,)), ((), ())), preferred_element_type=f32
        ).astype(bf16)
        rows = rows.reshape(2, half // 2, 2, -1, units)
        at = narrow + part * units
        for block, place in enumerate((level, 1 - level)):
            lines = pl.ds(place * (half // 2), half // 2)
            for odd in range(2):
                out_ref[lines, odd, :, at : at + units] = rows[block, :, odd]


def combine_far_body(half, acts_ref, *refs):
    near_refs, other_ref, out_ref = refs[:-2], refs[-2], refs[-1]
    pieces = []
    for distance, ref in enumerate(near_refs):
        pieces += [ref[0], other_ref[distance]]
    out_ref[...] = combined(half, acts_ref, pieces, out_ref.shape[0]).astype(bf16)


def combine_own_body(half, acts_ref, far_ref, *refs):
    out_ref = refs[-1]
    pieces = [ref[core] for ref in refs[:-1] for core in range(2)]
    total = combined(half, acts_ref, pieces, out_ref.shape[0])
    out_ref[...] = (total + far_ref[...].astype(f32)).astype(bf16)


def combined(half, acts_ref, pieces, tok):
    cap = pieces[0].shape[0]
    level, _ = level_and_side(half)
    diagonal = same_index(tok)
    ids, weights = read_meta(acts_ref)
    ids = ids.astype(jnp.int32) - half * level
    inside = (ids >= 0) & (ids < half)
    bin_of = jnp.where(inside, ids ^ place_in_half(half), -1).astype(f32)
    chosen = slot_choice(bin_of, half, cap).astype(f32).astype(bf16)
    rows = jnp.concatenate(pieces, axis=0)
    total = None
    for choice in range(2):
        picked = lax.dot_general(
            chosen[:, choice * tok : (choice + 1) * tok],
            rows,
            (((0,), (0,)), ((), ())),
            preferred_element_type=f32,
        )
        upright = jnp.sum(jnp.where(diagonal, weights[choice], 0.0), axis=1, keepdims=True)
        part = upright * picked
        total = part if total is None else total + part
    return total


def pick_grads_body(meta_ref, recv_ref, own_ref, send_ref):
    places, rows, total_wide = recv_ref.shape
    units = own_ref.shape[1]
    ids, _ = read_meta(meta_ref)
    chosen = slot_choice(ids, places, rows).astype(f32).astype(bf16)
    for part, out_ref in enumerate((own_ref, send_ref)):
        at = total_wide - (2 - part) * units
        picked = lax.dot_general(
            chosen,
            recv_ref[:, :, at : at + units].reshape(places * rows, units),
            (((0,), (0,)), ((), ())),
            preferred_element_type=f32,
        )
        out_ref[...] = picked.astype(out_ref.dtype)


def gate_grads_body(acts_ref, own_ref, got_ref, out_ref):
    tok = acts_ref.shape[0]
    units = own_ref.shape[1]
    for choice in range(2):
        at = 2 * choice * units
        lines = slice(choice * tok, (choice + 1) * tok)
        gate = acts_ref[:, at : at + units].astype(f32)
        up = acts_ref[:, at + units : at + 2 * units].astype(f32)
        grad = own_ref[lines, :] + got_ref[lines, :].astype(f32)
        sigmoid = jax.nn.sigmoid(gate)
        out_ref[:, at : at + units] = (
            grad * up * sigmoid * (1.0 + gate * (1.0 - sigmoid))
        ).astype(bf16)
        out_ref[:, at + units : at + 2 * units] = (grad * (gate * sigmoid)).astype(bf16)


def route_steps_body(source_ref, line_ref, recv_ref, out_ref):
    count, each, wide = out_ref.shape
    for k in range(count):
        line = pl.multiple_of(line_ref[k] * each, each)
        out_ref[k] = recv_ref[source_ref[k], pl.ds(line, each), 0:wide]


def place_steps_body(recv_ref, out_ref):
    groups, parts, sides, each, wide = recv_ref.shape
    for group in range(groups):
        for part in range(parts):
            for side in range(sides):
                at = (side * parts + part) * wide
                out_ref[group * each : (group + 1) * each, at : at + wide] = recv_ref[
                    group, part, side
                ]


def after(x, *others):
    return lax.optimization_barrier((x, *others))[0]


def mirrored_local(
    swap_pairs,
    expert_ids,
    route_weights,
    gate_up,
    grad_out,
    down_weight,
    first_moment,
    second_moment,
):
    places = lax.axis_size("expert")
    half = places // 2
    level, side = level_and_side(half)
    tok, top = expert_ids.shape
    units = down_weight.shape[1]
    wide = grad_out.shape[1]
    narrow = wide // 2
    cap = 2 * tok * top // places
    each = units // half
    across = [(k, (k + half) % places) for k in range(places)]
    beside = [(0, 1), (1, 0)]
    diagonal = [
        (2 * k + a, 2 * ((k + half) % places) + 1 - a) for k in range(places) for a in range(2)
    ]
    groups = [list(range(half)), list(range(half, places))]

    def mirror(x):
        return lax.ppermute(x, "expert", across)

    def neighbour(x):
        return lax.ppermute(x, "hidden", beside)

    def exchange(x):
        return lax.all_to_all(
            x, "expert", split_axis=0, concat_axis=0, tiled=True, axis_index_groups=groups
        )

    def shaped(*shape, dtype=bf16):
        return jax.ShapeDtypeStruct(shape, dtype)

    grads_far = [mirror(grad_out)]
    acts = gate_up.reshape(tok, 4 * units)
    hidden, noted = whole_call(
        prepare_body, (shaped(top * tok, units), shaped(top * tok + 16, units)), "prepare"
    )(acts, jnp.concatenate([expert_ids.astype(f32), route_weights], axis=1))
    noted_far = mirror(noted)
    hidden_beside = neighbour(hidden)
    hidden_diagonal = lax.ppermute(hidden, ("expert", "hidden"), diagonal)

    state = (down_weight[0], first_moment[0], second_moment[0])
    split = whole_call(split_body, shaped(1, units, wide), "split_state")
    weight_beside = neighbour(split(state[0]))
    first_beside = neighbour(split(after(state[1], hidden)))
    second_beside = neighbour(split(after(state[2], hidden)))

    row = wide + 2 * units
    pack = functools.partial(
        whole_call, functools.partial(pack_body, half), shaped(half, cap, row)
    )
    packed = pack("pack_own")(noted, hidden_beside, grad_out)
    recv = exchange(packed)

    packed_far = pack("pack_far", moved=HEAVY)(noted_far, hidden_diagonal, *grads_far)
    recv, packed_far, weight_beside, first_beside = lax.optimization_barrier(
        (recv, packed_far, weight_beside, first_beside)
    )
    recv_far = exchange(packed_far)
    recv_far, second_beside = lax.optimization_barrier((recv_far, second_beside))

    def forward(rows, block, shape, name):
        return whole_call(functools.partial(forward_body, half, block), shape, name)(
            rows, state[0], weight_beside
        )

    def at_distance(x, distance):
        return lax.ppermute(x, "expert", [(k, k ^ distance) for k in range(places)])

    def by_chip(outputs):
        return [outputs[0]] + [at_distance(outputs[k], 2 * k) for k in range(1, half // 2)]

    pairs = (shaped(2, cap, wide),) * (half // 2)
    cores = (shaped(half // 2, cap, wide),) * 2

    outputs_far = forward(recv_far, 1, pairs, "forward_far")
    steps = whole_call(
        functools.partial(update_body, half),
        shaped(half, 2, 2 * each, narrow + 2 * units),
        "update",
    )(recv, after(recv_far, outputs_far), *state, weight_beside, first_beside, second_beside)
    spread = lax.all_to_all(
        steps.reshape(places, 2 * each, narrow + 2 * units),
        "expert",
        split_axis=0,
        concat_axis=0,
        tiled=True,
    )

    near_far = by_chip(outputs_far)
    near_far, steps = lax.optimization_barrier((near_far, steps))
    crossing = whole_call(other_core_body, cores[0], "other_core_far")(*near_far)
    combined_send = whole_call(
        functools.partial(combine_far_body, half), shaped(tok, wide), "combine_far", 105_000_000
    )(noted_far, *near_far, at_distance(crossing, 1))
    combined_far = mirror(combined_send)
    keep_core, send_core = forward(after(recv, combined_send), 0, cores, "forward_own")
    joined = whole_call(join_cores_body, pairs, "join_cores")(
        keep_core, at_distance(send_core, 1)
    )
    near = by_chip(joined)

    partner = partner_table(swap_pairs, places)
    sides = jnp.tile(jnp.arange(2, dtype=jnp.int32), places)
    smem = pl.BlockSpec(memory_space=pltpu.SMEM)
    vmem = pl.BlockSpec(memory_space=pltpu.VMEM)
    routed = pl.pallas_call(
        route_steps_body,
        in_specs=[smem, smem, vmem],
        out_specs=vmem,
        out_shape=shaped(2 * places, each, narrow),
        name="route_steps",
        compiler_params=KERNEL_PARAMS,
    )(jnp.repeat(partner, 2).astype(jnp.int32), (sides ^ side).astype(jnp.int32), spread)
    placed = lax.all_to_all(
        after(routed, combined_send), ("expert", "hidden"), split_axis=0, concat_axis=0, tiled=True
    )

    rows_own, rows_send = whole_call(
        pick_grads_body,
        (shaped(top * tok, units, dtype=f32), shaped(top * tok, units)),
        "pick_grads",
        HEAVY,
    )(noted, spread)
    grad_gate_up = whole_call(gate_grads_body, shaped(tok, 4 * units), "gate_grads")(
        acts, rows_own, neighbour(rows_send)
    ).reshape(gate_up.shape)

    near, combined_far = lax.optimization_barrier((near, combined_far, rows_own))[:2]
    combined = whole_call(
        functools.partial(combine_own_body, half), shaped(tok, wide), "combine_own"
    )(noted, combined_far, *near)
    adam_step = whole_call(place_steps_body, shaped(units, 2 * wide), "place_steps")(
        placed.reshape(half, 2, 2, each, narrow)
    )
    return combined, grad_gate_up, adam_step[None]


def chosen_local(places, sides, *arrays):
    tok, top = arrays[1].shape
    units = arrays[5].shape[1]
    wide = arrays[4].shape[1]
    cap = 2 * tok * top // places
    fits = sides == 2 and top == 2 and places % 4 == 0 and places <= 256
    fits = fits and places * cap == 2 * tok * top and cap % 16 == 0
    fits = fits and wide % 256 == 0 and units == tok and tok % 128 == 0
    fits = fits and places & (places - 1) == 0 and (units // (places // 2)) % 16 == 0
    fits = fits and cap == 2 * (units // (places // 2))
    return mirrored_local(*arrays) if fits else general_local(*arrays)


def solution(mesh):
    placed = (
        P(),
        P("expert", None),
        P("expert", None),
        P("expert", None, None, "hidden"),
        P("expert", "hidden"),
        P("expert", "hidden", None),
        P("expert", "hidden", None),
        P("expert", "hidden", None),
    )
    return jax.shard_map(
        functools.partial(chosen_local, mesh.shape["expert"], mesh.shape["hidden"]),
        mesh=mesh,
        in_specs=placed,
        out_specs=(
            P("expert", "hidden"),
            P("expert", None, None, "hidden"),
            P("expert", "hidden", None),
        ),
        check_vma=False,
    )
```

```python
import functools
import jax
import jax.numpy as jnp
from jax import lax
from jax.experimental import pallas as pl
from jax.experimental.pallas import tpu as pltpu
from jax.sharding import PartitionSpec as P

first_decay = 0.9
second_decay = 0.95
adam_epsilon = 1e-08


def partner_table(swap_pairs, places):
    column = jnp.arange(places, dtype=jnp.int32)
    left = swap_pairs[:, 0]
    right = swap_pairs[:, 1]
    moved = jnp.where(left[:, None] == column[None, :], right[:, None] - column[None, :], 0)
    moved = moved + jnp.where(right[:, None] == column[None, :], left[:, None] - column[None, :], 0)
    return column + jnp.sum(moved, axis=0)


def relocate_state(weight_here, first_here, second_here, partner):
    places = partner.shape[0]
    shape_here = weight_here.shape
    spread = (
        lax.all_to_all(
            weight_here.reshape(places, -1), "expert", split_axis=0, concat_axis=0, tiled=True
        ),
        lax.all_to_all(
            first_here.reshape(places, -1), "expert", split_axis=0, concat_axis=0, tiled=True
        ),
        lax.all_to_all(
            second_here.reshape(places, -1), "expert", split_axis=0, concat_axis=0, tiled=True
        ),
    )
    ordered = tuple((jnp.take(member, partner, axis=0) for member in spread))
    collected = (
        lax.all_to_all(ordered[0], "expert", split_axis=0, concat_axis=0, tiled=True),
        lax.all_to_all(ordered[1], "expert", split_axis=0, concat_axis=0, tiled=True),
        lax.all_to_all(ordered[2], "expert", split_axis=0, concat_axis=0, tiled=True),
    )
    return tuple((member.reshape(shape_here) for member in collected))


def slot_numbers(destination, places, capacity):
    column = jnp.arange(places, dtype=jnp.int32)
    one_hot = (destination[:, None] == column[None, :]).astype(jnp.int32)
    before = jnp.cumsum(one_hot, axis=0) - one_hot
    earlier_count = jnp.sum(before * one_hot, axis=1)
    return destination * capacity + earlier_count


def general_local(
    swap_pairs,
    expert_ids,
    route_weights,
    gate_up,
    grad_out,
    down_weight,
    first_moment,
    second_moment,
):
    places = lax.axis_size("expert")
    tok_count, top_count = expert_ids.shape
    hid_dev = down_weight.shape[1]
    capacity = 2 * tok_count * top_count // places
    total_slots = places * capacity
    choice_count = tok_count * top_count
    partner = partner_table(swap_pairs, places)
    weight_here = down_weight[0]
    first_here = first_moment[0]
    second_here = second_moment[0]
    flat_ids = expert_ids.reshape(-1)
    column = jnp.arange(places, dtype=jnp.int32)
    weight_here, first_here, second_here = relocate_state(
        weight_here, first_here, second_here, partner
    )
    destination = jnp.sum(
        jnp.where(flat_ids[:, None] == column[None, :], partner[None, :], 0), axis=1
    )
    slot_index = slot_numbers(destination, places, capacity)
    choice_acts = gate_up.reshape(choice_count, 2 * hid_dev)
    scaled = (route_weights[:, :, None] * grad_out[:, None, :].astype(jnp.float32)).astype(
        jnp.bfloat16
    )
    scaled = scaled.reshape(choice_count, grad_out.shape[1])
    send_acts = jnp.zeros((total_slots, 2 * hid_dev), jnp.bfloat16).at[slot_index].set(choice_acts)
    send_grads = (
        jnp.zeros((total_slots, grad_out.shape[1]), jnp.bfloat16).at[slot_index].set(scaled)
    )
    recv_acts, recv_grads = (
        lax.all_to_all(
            send_acts.reshape(places, capacity, 2 * hid_dev),
            "expert",
            split_axis=0,
            concat_axis=0,
            tiled=True,
        ),
        lax.all_to_all(
            send_grads.reshape(places, capacity, grad_out.shape[1]),
            "expert",
            split_axis=0,
            concat_axis=0,
            tiled=True,
        ),
    )
    recv_acts = recv_acts.reshape(total_slots, 2 * hid_dev)
    recv_grads = recv_grads.reshape(total_slots, grad_out.shape[1])
    gate_pre = recv_acts[:, :hid_dev].astype(jnp.float32)
    up_pre = recv_acts[:, hid_dev:].astype(jnp.float32)
    sigmoid_gate = jax.nn.sigmoid(gate_pre)
    silu_gate = gate_pre * sigmoid_gate
    hidden = (silu_gate * up_pre).astype(jnp.bfloat16)
    partial_value = jnp.dot(hidden, weight_here, preferred_element_type=jnp.float32)
    summed = lax.psum_scatter(
        partial_value.astype(jnp.bfloat16), "hidden", scatter_dimension=1, tiled=True
    ).astype(jnp.float32)
    returned = lax.all_to_all(
        summed.reshape(places, capacity, summed.shape[1]).astype(jnp.bfloat16),
        "expert",
        split_axis=0,
        concat_axis=0,
        tiled=True,
    ).astype(jnp.float32)
    per_choice = jnp.take(returned.reshape(total_slots, summed.shape[1]), slot_index, axis=0)
    per_choice = per_choice.reshape(tok_count, top_count, summed.shape[1])
    combined = jnp.einsum("tk,tkd->td", route_weights, per_choice).astype(jnp.bfloat16)
    portion = lax.all_gather(recv_grads, "hidden", axis=1, tiled=True)
    grad_hidden = lax.dot_general(
        portion, weight_here, (((1,), (1,)), ((), ())), preferred_element_type=jnp.float32
    )
    product_block = lax.dot_general(
        hidden, portion, (((0,), (0,)), ((), ())), preferred_element_type=jnp.float32
    )
    grad_weight = product_block
    grad_hidden, grad_weight = (grad_hidden, grad_weight)
    grad_gate = grad_hidden * up_pre * sigmoid_gate * (1.0 + gate_pre * (1.0 - sigmoid_gate))
    grad_up = grad_hidden * silu_gate
    grad_rows = jnp.concatenate([grad_gate, grad_up], axis=1).astype(jnp.bfloat16)
    returned_grads = lax.all_to_all(
        grad_rows.reshape(places, capacity, 2 * hid_dev),
        "expert",
        split_axis=0,
        concat_axis=0,
        tiled=True,
    )
    grad_gate_up = jnp.take(returned_grads.reshape(total_slots, 2 * hid_dev), slot_index, axis=0)
    grad_gate_up = grad_gate_up.reshape(tok_count, top_count, 2, hid_dev)
    first_new = first_decay * first_here.astype(jnp.float32) + (1.0 - first_decay) * grad_weight
    second_new = (
        second_decay * second_here.astype(jnp.float32)
        + (1.0 - second_decay) * grad_weight * grad_weight
    )
    update = (first_new / (jnp.sqrt(second_new) + adam_epsilon)).astype(jnp.bfloat16)
    return (combined, grad_gate_up, update[None])


bf16 = jnp.bfloat16
f32 = jnp.float32
HEAVY = 10_000_000_000
KERNEL_PARAMS = pltpu.CompilerParams(vmem_limit_bytes=40 * 1024 * 1024)


def whole_call(body, out_shape, name, moved=None):
    cost = None if moved is None else pl.CostEstimate(flops=100 * moved, bytes_accessed=moved, transcendentals=0)
    return pl.pallas_call(
        body, out_shape=out_shape, name=name, compiler_params=KERNEL_PARAMS, cost_estimate=cost
    )


def level_and_side(half):
    return lax.axis_index("expert") // half, lax.axis_index("hidden")


def columns_at(ref, index, wide):
    return ref[:, pl.ds(pl.multiple_of(index * wide, wide), wide)]


def same_index(size):
    first = lax.broadcasted_iota(jnp.int32, (size, size), 0)
    second = lax.broadcasted_iota(jnp.int32, (size, size), 1)
    return first == second


def prepare_body(acts_ref, choices_ref, hidden_ref, far_ref):
    tok = acts_ref.shape[0]
    units = acts_ref.shape[1] // 4
    for choice in range(2):
        at = 2 * choice * units
        gate = acts_ref[:, at : at + units].astype(f32)
        up = acts_ref[:, at + units : at + 2 * units].astype(f32)
        value = (gate * jax.nn.sigmoid(gate) * up).astype(bf16)
        hidden_ref[choice * tok : (choice + 1) * tok, :] = value
        far_ref[choice * tok : (choice + 1) * tok, :] = value
    ids, weights = choices_ref[:, 0:2], choices_ref[:, 2:4]
    high = weights.astype(bf16)
    middle = (weights - high.astype(f32)).astype(bf16)
    low = (weights - high.astype(f32) - middle.astype(f32)).astype(bf16)
    unit = same_index(tok).astype(f32).astype(bf16)
    pieces = [
        lax.dot_general(piece, unit, (((0,), (0,)), ((), ())), preferred_element_type=f32)
        for piece in (ids.astype(bf16), high, middle, low)
    ]
    blank = jnp.zeros((16 - 8, tok), f32)
    far_ref[2 * tok : 2 * tok + 16, :] = jnp.concatenate(pieces + [blank], axis=0).astype(bf16)


def split_body(ref, keep_ref, other_ref):
    side = lax.axis_index("hidden")
    wide = ref.shape[1] // 2
    keep_ref[0] = columns_at(ref, side, wide)
    other_ref[0] = columns_at(ref, 1 - side, wide)


def read_meta(ref):
    tok = ref.shape[1]
    meta = ref[2 * tok : 2 * tok + 16, :].astype(f32)
    ids = jnp.concatenate([meta[0:1, :], meta[1:2, :]], axis=1)
    weights = [
        meta[2 + k : 3 + k, :] + meta[4 + k : 5 + k, :] + meta[6 + k : 7 + k, :] for k in range(2)
    ]
    return ids, weights


def slot_choice(bin_of, bins, cap):
    count = bin_of.shape[1]
    column = lax.broadcasted_iota(jnp.int32, (bins, count), 0).astype(f32)
    one_hot = (bin_of == column).astype(f32)
    first = lax.broadcasted_iota(jnp.int32, (count, count), 0)
    second = lax.broadcasted_iota(jnp.int32, (count, count), 1)
    earlier = (first < second).astype(f32).astype(bf16)
    rank = jnp.dot(one_hot.astype(bf16), earlier, preferred_element_type=f32)
    slot = jnp.sum(one_hot * (rank + column * cap + 1.0), axis=0, keepdims=True) - 1.0
    return slot == lax.broadcasted_iota(jnp.int32, (bins * cap, count), 0).astype(f32)


def pack_body(half, acts_ref, beside_ref, *refs):
    out_ref = refs[-1]
    bins, cap, _ = out_ref.shape
    units = beside_ref.shape[1]
    grads = jnp.concatenate([ref[...] for ref in refs[:-1]], axis=0)
    tok, wide = grads.shape
    level, _ = level_and_side(half)
    ids, weights = read_meta(acts_ref)
    chosen = slot_choice(ids - (half * level).astype(f32), bins, cap)
    weights = jnp.concatenate(weights, axis=1)
    factor = jnp.sum(jnp.where(chosen, weights, 0.0), axis=1, keepdims=True)
    one_hot = chosen.astype(f32)
    by_token = (one_hot[:, :tok] + one_hot[:, tok:]).astype(bf16)
    rows = jnp.dot(by_token, grads, preferred_element_type=f32)
    out_ref[:, :, 0:wide] = (rows * factor).astype(bf16).reshape(bins, cap, wide)
    for side, ref in enumerate((acts_ref, beside_ref)):
        at = wide + side * units
        acts = jnp.dot(
            one_hot.astype(bf16), ref[0 : 2 * tok, :], preferred_element_type=f32
        )
        out_ref[:, :, at : at + units] = acts.astype(bf16).reshape(bins, cap, units)


def rows_of(ref, start, size):
    sources, cap, _ = ref.shape
    return ref[:, :, start : start + size].reshape(sources * cap, size)


def place_in_half(half):
    return lax.rem(lax.axis_index("expert"), half)


def output_rows(half, recv_ref, weight_ref, beside_ref, cap):
    units, wide = weight_ref.shape[1:]
    me = place_in_half(half)
    acts = jnp.concatenate([recv_ref[me ^ r, :, wide:] for r in range(half)], axis=0)
    total = jnp.dot(acts[:, :units], weight_ref[0], preferred_element_type=f32)
    total = total + jnp.dot(acts[:, units:], beside_ref[0], preferred_element_type=f32)
    return total.astype(bf16).reshape(half // 2, 2, cap, wide)


def forward_far_body(half, recv_ref, weight_ref, beside_ref, *out_refs):
    total = output_rows(half, recv_ref, weight_ref, beside_ref, out_refs[0].shape[1])
    for distance, ref in enumerate(out_refs):
        ref[...] = total[distance]


def forward_own_body(half, recv_ref, weight_ref, beside_ref, grads_ref, mirror_ref, *out_refs):
    total = output_rows(half, recv_ref, weight_ref, beside_ref, out_refs[0].shape[1])
    wide = total.shape[3]
    units = grads_ref.shape[2]
    me = place_in_half(half)
    for core, out_ref in enumerate(out_refs):
        out_ref[:, :, 0:wide] = total[:, core]
        for distance in range(half // 2):
            source = me ^ (2 * distance + core)
            out_ref[distance, :, wide : wide + units] = grads_ref[source]
            out_ref[distance, :, wide + units :] = mirror_ref[source]


def grad_rows_body(recv_ref, weight_ref, beside_ref, out_ref):
    units, wide = weight_ref.shape[1:]
    scaled = rows_of(recv_ref, 0, wide)
    for part, weight in enumerate((weight_ref[0], beside_ref[0])):
        rows = lax.dot_general(
            scaled, weight, (((1,), (1,)), ((), ())), preferred_element_type=f32
        )
        out_ref[:, :, part * units : (part + 1) * units] = rows.astype(bf16).reshape(
            out_ref.shape[:2] + (units,)
        )


def join_cores_body(keep_ref, got_ref, *out_refs):
    for distance, ref in enumerate(out_refs):
        ref[0] = keep_ref[distance]
        ref[1] = got_ref[distance]


def other_core_body(*refs):
    out_ref = refs[-1]
    for distance, ref in enumerate(refs[:-1]):
        out_ref[distance] = ref[1]


def update_body(
    recv_ref, far_ref, first_ref, second_ref, first_beside, second_beside, out_ref
):
    _, units, wide = first_beside.shape
    groups = out_ref.shape[0]
    narrow = wide // 2
    each = units // groups
    for part in range(2):
        grads = None
        for ref in (recv_ref, far_ref):
            more = lax.dot_general(
                rows_of(ref, wide, 2 * units),
                rows_of(ref, part * narrow, narrow),
                (((0,), (0,)), ((), ())),
                preferred_element_type=f32,
            )
            grads = more if grads is None else grads + more
        for side in range(2):
            own = (first_ref, second_ref) if side == 0 else (first_beside, second_beside)
            moments = [ref[0, :, part * narrow : (part + 1) * narrow] for ref in own]
            grad = grads[side * units : (side + 1) * units]
            first = first_decay * moments[0].astype(f32) + (1.0 - first_decay) * grad
            second = second_decay * moments[1].astype(f32)
            second = second + (1.0 - second_decay) * grad * grad
            root = second * lax.rsqrt(second) + adam_epsilon
            step = (first * pl.reciprocal(root, approx=True)).astype(bf16)
            out_ref[:, part, side * each : (side + 1) * each, 0:narrow] = step.reshape(
                groups, each, narrow
            )


def combine_far_body(half, acts_ref, *refs):
    near_refs, other_ref, out_ref = refs[:-2], refs[-2], refs[-1]
    pieces = []
    for distance, ref in enumerate(near_refs):
        pieces += [ref[0], other_ref[distance]]
    out_ref[...] = combined(half, acts_ref, pieces, out_ref.shape[0]).astype(bf16)


def combine_own_body(half, acts_ref, chosen_ref, far_ref, *refs):
    out_ref = refs[-1]
    tok, wide = out_ref.shape
    pieces = [ref[core, :, 0:wide] for ref in refs[:-1] for core in range(2)]
    _, weights = read_meta(acts_ref)
    total = weighted_sum(chosen_ref[...], weights, jnp.concatenate(pieces, axis=0), tok)
    out_ref[...] = (total + far_ref[...].astype(f32)).astype(bf16)


def choose_body(half, acts_ref, chosen_ref):
    ids, _ = read_meta(acts_ref)
    chosen_ref[...] = returned_choice(half, ids, chosen_ref.shape[0] // half)


def returned_choice(half, ids, cap):
    level, _ = level_and_side(half)
    ids = ids.astype(jnp.int32) - half * level
    inside = (ids >= 0) & (ids < half)
    bin_of = jnp.where(inside, ids ^ place_in_half(half), -1).astype(f32)
    return slot_choice(bin_of, half, cap).astype(f32).astype(bf16)


def weighted_sum(chosen, weights, rows, tok):
    diagonal = same_index(tok)
    total = None
    for choice in range(2):
        picked = lax.dot_general(
            chosen[:, choice * tok : (choice + 1) * tok],
            rows,
            (((0,), (0,)), ((), ())),
            preferred_element_type=f32,
        )
        upright = jnp.sum(jnp.where(diagonal, weights[choice], 0.0), axis=1, keepdims=True)
        part = upright * picked
        total = part if total is None else total + part
    return total


def combined(half, acts_ref, pieces, tok):
    ids, weights = read_meta(acts_ref)
    chosen = returned_choice(half, ids, pieces[0].shape[0])
    return weighted_sum(chosen, weights, jnp.concatenate(pieces, axis=0), tok)


def pick_grads_body(half, meta_ref, *refs):
    near_refs, own_ref, send_ref = refs[:-2], refs[-2], refs[-1]
    units = own_ref.shape[1]
    _, cap, total_wide = near_refs[0].shape
    wide = total_wide - 4 * units
    level, _ = level_and_side(half)
    ids, _ = read_meta(meta_ref)
    upper = (ids >= half).astype(jnp.int32)
    place = (ids.astype(jnp.int32) - half * upper) ^ place_in_half(half)
    bin_of = (2 * place + (upper ^ level)).astype(f32)
    chosen = slot_choice(bin_of, 2 * half, cap).astype(f32).astype(bf16)
    for part, out_ref in enumerate((own_ref, send_ref)):
        pieces = []
        for ref in near_refs:
            for core in range(2):
                for expert in range(2):
                    at = wide + (2 * expert + part) * units
                    pieces.append(ref[core, :, at : at + units])
        picked = lax.dot_general(
            chosen,
            jnp.concatenate(pieces, axis=0),
            (((0,), (0,)), ((), ())),
            preferred_element_type=f32,
        )
        out_ref[...] = picked.astype(out_ref.dtype)


def gate_grads_body(acts_ref, own_ref, got_ref, out_ref):
    tok = acts_ref.shape[0]
    units = own_ref.shape[1]
    for choice in range(2):
        at = 2 * choice * units
        lines = slice(choice * tok, (choice + 1) * tok)
        gate = acts_ref[:, at : at + units].astype(f32)
        up = acts_ref[:, at + units : at + 2 * units].astype(f32)
        grad = own_ref[lines, :] + got_ref[lines, :].astype(f32)
        sigmoid = jax.nn.sigmoid(gate)
        out_ref[:, at : at + units] = (
            grad * up * sigmoid * (1.0 + gate * (1.0 - sigmoid))
        ).astype(bf16)
        out_ref[:, at + units : at + 2 * units] = (grad * (gate * sigmoid)).astype(bf16)


def route_steps_body(source_ref, line_ref, recv_ref, out_ref):
    count, each, wide = out_ref.shape
    for k in range(count):
        line = pl.multiple_of(line_ref[k] * each, each)
        out_ref[k] = recv_ref[source_ref[k], pl.ds(line, each), 0:wide]


def place_steps_body(recv_ref, out_ref):
    groups, parts, sides, each, wide = recv_ref.shape
    for group in range(groups):
        for part in range(parts):
            for side in range(sides):
                at = (side * parts + part) * wide
                out_ref[group * each : (group + 1) * each, at : at + wide] = recv_ref[
                    group, part, side
                ]


def after(x, *others):
    return lax.optimization_barrier((x, *others))[0]


def mirrored_local(
    swap_pairs,
    expert_ids,
    route_weights,
    gate_up,
    grad_out,
    down_weight,
    first_moment,
    second_moment,
):
    places = lax.axis_size("expert")
    half = places // 2
    level, side = level_and_side(half)
    tok, top = expert_ids.shape
    units = down_weight.shape[1]
    wide = grad_out.shape[1]
    narrow = wide // 2
    cap = 2 * tok * top // places
    each = units // half
    across = [(k, (k + half) % places) for k in range(places)]
    beside = [(0, 1), (1, 0)]
    diagonal = [
        (2 * k + a, 2 * ((k + half) % places) + 1 - a) for k in range(places) for a in range(2)
    ]
    groups = [list(range(half)), list(range(half, places))]

    def mirror(x):
        return lax.ppermute(x, "expert", across)

    def neighbour(x):
        return lax.ppermute(x, "hidden", beside)

    def exchange(x):
        return lax.all_to_all(
            x, "expert", split_axis=0, concat_axis=0, tiled=True, axis_index_groups=groups
        )

    def shaped(*shape, dtype=bf16):
        return jax.ShapeDtypeStruct(shape, dtype)

    grads_far = [mirror(grad_out)]
    acts = gate_up.reshape(tok, 4 * units)
    hidden, noted = whole_call(
        prepare_body, (shaped(top * tok, units), shaped(top * tok + 16, units)), "prepare"
    )(acts, jnp.concatenate([expert_ids.astype(f32), route_weights], axis=1))
    noted_far = mirror(noted)
    hidden_beside = neighbour(hidden)
    hidden_diagonal = lax.ppermute(hidden, ("expert", "hidden"), diagonal)

    split = whole_call(split_body, (shaped(1, units, wide),) * 2, "split_state")
    weight, weight_other = split(down_weight[0])
    first, first_other = split(after(first_moment[0], hidden))
    second, second_other = split(after(second_moment[0], hidden))
    weight_beside = neighbour(weight_other)
    first_beside = neighbour(first_other)
    second_beside = neighbour(second_other)

    row = wide + 2 * units
    pack = functools.partial(
        whole_call, functools.partial(pack_body, half), shaped(half, cap, row)
    )
    packed = pack("pack_own")(noted, hidden_beside, grad_out)
    recv = exchange(packed)

    packed_far = pack("pack_far", moved=HEAVY)(noted_far, hidden_diagonal, *grads_far)
    recv, packed_far, weight_beside, first_beside = lax.optimization_barrier(
        (recv, packed_far, weight_beside, first_beside)
    )
    recv_far = exchange(packed_far)
    grad_rows = whole_call(grad_rows_body, shaped(half, cap, 2 * units), "grad_rows")
    rows_own = grad_rows(recv, weight, weight_beside)
    recv_far, second_beside, rows_own = lax.optimization_barrier(
        (recv_far, second_beside, rows_own)
    )

    def at_distance(x, distance):
        return lax.ppermute(x, "expert", [(k, k ^ distance) for k in range(places)])

    def by_chip(outputs):
        return [outputs[0]] + [at_distance(outputs[k], 2 * k) for k in range(1, half // 2)]

    pairs = (shaped(2, cap, wide),) * (half // 2)
    extended = wide + 4 * units
    outputs_far = whole_call(functools.partial(forward_far_body, half), pairs, "forward_far")(
        recv_far, weight, weight_beside
    )

    rows_send = grad_rows(recv_far, weight, weight_beside)
    rows_mirror = mirror(rows_send)
    steps = whole_call(update_body, shaped(half, 2, 2 * each, narrow), "update")(
        recv, after(recv_far, outputs_far, rows_send), first, second, first_beside, second_beside
    )
    spread = lax.all_to_all(
        steps.reshape(places, 2 * each, narrow),
        "expert",
        split_axis=0,
        concat_axis=0,
        tiled=True,
    )

    near_far = by_chip(outputs_far)
    near_far, rows_mirror = lax.optimization_barrier((near_far, rows_mirror, steps))[:2]
    crossing = whole_call(
        other_core_body, shaped(half // 2, cap, wide), "other_core_far"
    )(*near_far)
    combined_send = whole_call(
        functools.partial(combine_far_body, half), shaped(tok, wide), "combine_far", 55_000_000
    )(noted_far, *near_far, at_distance(crossing, 1))
    combined_far = mirror(combined_send)
    keep_core, send_core = whole_call(
        functools.partial(forward_own_body, half),
        (shaped(half // 2, cap, extended),) * 2,
        "forward_own",
    )(after(recv, combined_send), weight, weight_beside, rows_own, rows_mirror)
    joined = whole_call(join_cores_body, (shaped(2, cap, extended),) * (half // 2), "join_cores")(
        keep_core, at_distance(send_core, 1)
    )
    near = by_chip(joined)

    partner = partner_table(swap_pairs, places)
    sides = jnp.tile(jnp.arange(2, dtype=jnp.int32), places)
    smem = pl.BlockSpec(memory_space=pltpu.SMEM)
    vmem = pl.BlockSpec(memory_space=pltpu.VMEM)
    routed = pl.pallas_call(
        route_steps_body,
        in_specs=[smem, smem, vmem],
        out_specs=vmem,
        out_shape=shaped(2 * places, each, narrow),
        name="route_steps",
        compiler_params=KERNEL_PARAMS,
    )(jnp.repeat(partner, 2).astype(jnp.int32), (sides ^ side).astype(jnp.int32), spread)
    placed = lax.all_to_all(
        after(routed, combined_send), ("expert", "hidden"), split_axis=0, concat_axis=0, tiled=True
    )

    chosen = whole_call(
        functools.partial(choose_body, half), shaped(half * cap, top * tok), "choose", HEAVY
    )(after(noted, spread))
    near, combined_far, chosen = lax.optimization_barrier((near, combined_far, chosen))
    grads_own, grads_send = whole_call(
        functools.partial(pick_grads_body, half),
        (shaped(top * tok, units, dtype=f32), shaped(top * tok, units)),
        "pick_grads",
    )(noted, *near)
    grad_gate_up = whole_call(gate_grads_body, shaped(tok, 4 * units), "gate_grads")(
        acts, grads_own, neighbour(grads_send)
    ).reshape(gate_up.shape)
    combined = whole_call(
        functools.partial(combine_own_body, half), shaped(tok, wide), "combine_own"
    )(noted, chosen, combined_far, *near)
    adam_step = whole_call(place_steps_body, shaped(units, 2 * wide), "place_steps")(
        placed.reshape(half, 2, 2, each, narrow)
    )
    return combined, grad_gate_up, adam_step[None]


def chosen_local(places, sides, *arrays):
    tok, top = arrays[1].shape
    units = arrays[5].shape[1]
    wide = arrays[4].shape[1]
    cap = 2 * tok * top // places
    fits = sides == 2 and top == 2 and places % 4 == 0 and places <= 256
    fits = fits and places * cap == 2 * tok * top and cap % 16 == 0
    fits = fits and wide % 256 == 0 and units == tok and tok % 128 == 0
    fits = fits and places & (places - 1) == 0 and (units // (places // 2)) % 16 == 0
    fits = fits and cap == 2 * (units // (places // 2))
    return mirrored_local(*arrays) if fits else general_local(*arrays)


def solution(mesh):
    placed = (
        P(),
        P("expert", None),
        P("expert", None),
        P("expert", None, None, "hidden"),
        P("expert", "hidden"),
        P("expert", "hidden", None),
        P("expert", "hidden", None),
        P("expert", "hidden", None),
    )
    return jax.shard_map(
        functools.partial(chosen_local, mesh.shape["expert"], mesh.shape["hidden"]),
        mesh=mesh,
        in_specs=placed,
        out_specs=(
            P("expert", "hidden"),
            P("expert", None, None, "hidden"),
            P("expert", "hidden", None),
        ),
        check_vma=False,
    )
```

```python
import functools
import jax
import jax.numpy as jnp
from jax import lax
from jax.experimental import pallas as pl
from jax.experimental.pallas import tpu as pltpu
from jax.sharding import PartitionSpec as P

first_decay = 0.9
second_decay = 0.95
adam_epsilon = 1e-08


def partner_table(swap_pairs, places):
    column = jnp.arange(places, dtype=jnp.int32)
    left = swap_pairs[:, 0]
    right = swap_pairs[:, 1]
    moved = jnp.where(left[:, None] == column[None, :], right[:, None] - column[None, :], 0)
    moved = moved + jnp.where(right[:, None] == column[None, :], left[:, None] - column[None, :], 0)
    return column + jnp.sum(moved, axis=0)


def relocate_state(weight_here, first_here, second_here, partner):
    places = partner.shape[0]
    shape_here = weight_here.shape
    spread = (
        lax.all_to_all(
            weight_here.reshape(places, -1), "expert", split_axis=0, concat_axis=0, tiled=True
        ),
        lax.all_to_all(
            first_here.reshape(places, -1), "expert", split_axis=0, concat_axis=0, tiled=True
        ),
        lax.all_to_all(
            second_here.reshape(places, -1), "expert", split_axis=0, concat_axis=0, tiled=True
        ),
    )
    ordered = tuple((jnp.take(member, partner, axis=0) for member in spread))
    collected = (
        lax.all_to_all(ordered[0], "expert", split_axis=0, concat_axis=0, tiled=True),
        lax.all_to_all(ordered[1], "expert", split_axis=0, concat_axis=0, tiled=True),
        lax.all_to_all(ordered[2], "expert", split_axis=0, concat_axis=0, tiled=True),
    )
    return tuple((member.reshape(shape_here) for member in collected))


def slot_numbers(destination, places, capacity):
    column = jnp.arange(places, dtype=jnp.int32)
    one_hot = (destination[:, None] == column[None, :]).astype(jnp.int32)
    before = jnp.cumsum(one_hot, axis=0) - one_hot
    earlier_count = jnp.sum(before * one_hot, axis=1)
    return destination * capacity + earlier_count


def general_local(
    swap_pairs,
    expert_ids,
    route_weights,
    gate_up,
    grad_out,
    down_weight,
    first_moment,
    second_moment,
):
    places = lax.axis_size("expert")
    tok_count, top_count = expert_ids.shape
    hid_dev = down_weight.shape[1]
    capacity = 2 * tok_count * top_count // places
    total_slots = places * capacity
    choice_count = tok_count * top_count
    partner = partner_table(swap_pairs, places)
    weight_here = down_weight[0]
    first_here = first_moment[0]
    second_here = second_moment[0]
    flat_ids = expert_ids.reshape(-1)
    column = jnp.arange(places, dtype=jnp.int32)
    weight_here, first_here, second_here = relocate_state(
        weight_here, first_here, second_here, partner
    )
    destination = jnp.sum(
        jnp.where(flat_ids[:, None] == column[None, :], partner[None, :], 0), axis=1
    )
    slot_index = slot_numbers(destination, places, capacity)
    choice_acts = gate_up.reshape(choice_count, 2 * hid_dev)
    scaled = (route_weights[:, :, None] * grad_out[:, None, :].astype(jnp.float32)).astype(
        jnp.bfloat16
    )
    scaled = scaled.reshape(choice_count, grad_out.shape[1])
    send_acts = jnp.zeros((total_slots, 2 * hid_dev), jnp.bfloat16).at[slot_index].set(choice_acts)
    send_grads = (
        jnp.zeros((total_slots, grad_out.shape[1]), jnp.bfloat16).at[slot_index].set(scaled)
    )
    recv_acts, recv_grads = (
        lax.all_to_all(
            send_acts.reshape(places, capacity, 2 * hid_dev),
            "expert",
            split_axis=0,
            concat_axis=0,
            tiled=True,
        ),
        lax.all_to_all(
            send_grads.reshape(places, capacity, grad_out.shape[1]),
            "expert",
            split_axis=0,
            concat_axis=0,
            tiled=True,
        ),
    )
    recv_acts = recv_acts.reshape(total_slots, 2 * hid_dev)
    recv_grads = recv_grads.reshape(total_slots, grad_out.shape[1])
    gate_pre = recv_acts[:, :hid_dev].astype(jnp.float32)
    up_pre = recv_acts[:, hid_dev:].astype(jnp.float32)
    sigmoid_gate = jax.nn.sigmoid(gate_pre)
    silu_gate = gate_pre * sigmoid_gate
    hidden = (silu_gate * up_pre).astype(jnp.bfloat16)
    partial_value = jnp.dot(hidden, weight_here, preferred_element_type=jnp.float32)
    summed = lax.psum_scatter(
        partial_value.astype(jnp.bfloat16), "hidden", scatter_dimension=1, tiled=True
    ).astype(jnp.float32)
    returned = lax.all_to_all(
        summed.reshape(places, capacity, summed.shape[1]).astype(jnp.bfloat16),
        "expert",
        split_axis=0,
        concat_axis=0,
        tiled=True,
    ).astype(jnp.float32)
    per_choice = jnp.take(returned.reshape(total_slots, summed.shape[1]), slot_index, axis=0)
    per_choice = per_choice.reshape(tok_count, top_count, summed.shape[1])
    combined = jnp.einsum("tk,tkd->td", route_weights, per_choice).astype(jnp.bfloat16)
    portion = lax.all_gather(recv_grads, "hidden", axis=1, tiled=True)
    grad_hidden = lax.dot_general(
        portion, weight_here, (((1,), (1,)), ((), ())), preferred_element_type=jnp.float32
    )
    product_block = lax.dot_general(
        hidden, portion, (((0,), (0,)), ((), ())), preferred_element_type=jnp.float32
    )
    grad_weight = product_block
    grad_hidden, grad_weight = (grad_hidden, grad_weight)
    grad_gate = grad_hidden * up_pre * sigmoid_gate * (1.0 + gate_pre * (1.0 - sigmoid_gate))
    grad_up = grad_hidden * silu_gate
    grad_rows = jnp.concatenate([grad_gate, grad_up], axis=1).astype(jnp.bfloat16)
    returned_grads = lax.all_to_all(
        grad_rows.reshape(places, capacity, 2 * hid_dev),
        "expert",
        split_axis=0,
        concat_axis=0,
        tiled=True,
    )
    grad_gate_up = jnp.take(returned_grads.reshape(total_slots, 2 * hid_dev), slot_index, axis=0)
    grad_gate_up = grad_gate_up.reshape(tok_count, top_count, 2, hid_dev)
    first_new = first_decay * first_here.astype(jnp.float32) + (1.0 - first_decay) * grad_weight
    second_new = (
        second_decay * second_here.astype(jnp.float32)
        + (1.0 - second_decay) * grad_weight * grad_weight
    )
    update = (first_new / (jnp.sqrt(second_new) + adam_epsilon)).astype(jnp.bfloat16)
    return (combined, grad_gate_up, update[None])


bf16 = jnp.bfloat16
f32 = jnp.float32
HEAVY = 10_000_000_000
KERNEL_PARAMS = pltpu.CompilerParams(vmem_limit_bytes=40 * 1024 * 1024)


def whole_call(body, out_shape, name, moved=None):
    cost = None if moved is None else pl.CostEstimate(flops=100 * moved, bytes_accessed=moved, transcendentals=0)
    return pl.pallas_call(
        body, out_shape=out_shape, name=name, compiler_params=KERNEL_PARAMS, cost_estimate=cost
    )


def level_and_side(half):
    return lax.axis_index("expert") // half, lax.axis_index("hidden")


def columns_at(ref, index, wide):
    return ref[:, pl.ds(pl.multiple_of(index * wide, wide), wide)]


def same_index(size):
    first = lax.broadcasted_iota(jnp.int32, (size, size), 0)
    second = lax.broadcasted_iota(jnp.int32, (size, size), 1)
    return first == second


def prepare_body(acts_ref, choices_ref, hidden_ref, far_ref):
    tok = acts_ref.shape[0]
    units = acts_ref.shape[1] // 4
    for choice in range(2):
        at = 2 * choice * units
        gate = acts_ref[:, at : at + units].astype(f32)
        up = acts_ref[:, at + units : at + 2 * units].astype(f32)
        value = (gate * jax.nn.sigmoid(gate) * up).astype(bf16)
        hidden_ref[choice * tok : (choice + 1) * tok, :] = value
        far_ref[choice * tok : (choice + 1) * tok, :] = value
    ids, weights = choices_ref[:, 0:2], choices_ref[:, 2:4]
    high = weights.astype(bf16)
    middle = (weights - high.astype(f32)).astype(bf16)
    low = (weights - high.astype(f32) - middle.astype(f32)).astype(bf16)
    unit = same_index(tok).astype(f32).astype(bf16)
    pieces = [
        lax.dot_general(piece, unit, (((0,), (0,)), ((), ())), preferred_element_type=f32)
        for piece in (ids.astype(bf16), high, middle, low)
    ]
    blank = jnp.zeros((16 - 8, tok), f32)
    far_ref[2 * tok : 2 * tok + 16, :] = jnp.concatenate(pieces + [blank], axis=0).astype(bf16)


def split_body(ref, keep_ref, other_ref):
    side = lax.axis_index("hidden")
    wide = ref.shape[1] // 2
    keep_ref[0] = columns_at(ref, side, wide)
    other_ref[0] = columns_at(ref, 1 - side, wide)


def read_meta(ref):
    tok = ref.shape[1]
    meta = ref[2 * tok : 2 * tok + 16, :].astype(f32)
    ids = jnp.concatenate([meta[0:1, :], meta[1:2, :]], axis=1)
    weights = [
        meta[2 + k : 3 + k, :] + meta[4 + k : 5 + k, :] + meta[6 + k : 7 + k, :] for k in range(2)
    ]
    return ids, weights


def slot_choice(bin_of, bins, cap):
    count = bin_of.shape[1]
    column = lax.broadcasted_iota(jnp.int32, (bins, count), 0).astype(f32)
    one_hot = (bin_of == column).astype(f32)
    first = lax.broadcasted_iota(jnp.int32, (count, count), 0)
    second = lax.broadcasted_iota(jnp.int32, (count, count), 1)
    earlier = (first < second).astype(f32).astype(bf16)
    rank = jnp.dot(one_hot.astype(bf16), earlier, preferred_element_type=f32)
    slot = jnp.sum(one_hot * (rank + column * cap + 1.0), axis=0, keepdims=True) - 1.0
    return slot == lax.broadcasted_iota(jnp.int32, (bins * cap, count), 0).astype(f32)


def pack_body(half, acts_ref, beside_ref, *refs):
    out_ref = refs[-1]
    bins, cap, _ = out_ref.shape
    units = beside_ref.shape[1]
    grads = jnp.concatenate([ref[...] for ref in refs[:-1]], axis=0)
    tok, wide = grads.shape
    level, _ = level_and_side(half)
    ids, weights = read_meta(acts_ref)
    chosen = slot_choice(ids - (half * level).astype(f32), bins, cap)
    weights = jnp.concatenate(weights, axis=1)
    factor = jnp.sum(jnp.where(chosen, weights, 0.0), axis=1, keepdims=True)
    one_hot = chosen.astype(f32)
    by_token = (one_hot[:, :tok] + one_hot[:, tok:]).astype(bf16)
    rows = jnp.dot(by_token, grads, preferred_element_type=f32)
    out_ref[:, :, 0:wide] = (rows * factor).astype(bf16).reshape(bins, cap, wide)
    for side, ref in enumerate((acts_ref, beside_ref)):
        at = wide + side * units
        acts = jnp.dot(
            one_hot.astype(bf16), ref[0 : 2 * tok, :], preferred_element_type=f32
        )
        out_ref[:, :, at : at + units] = acts.astype(bf16).reshape(bins, cap, units)


def rows_of(ref, start, size):
    sources, cap, _ = ref.shape
    return ref[:, :, start : start + size].reshape(sources * cap, size)


def place_in_half(half):
    return lax.rem(lax.axis_index("expert"), half)


def output_rows(half, recv_ref, weight_ref, beside_ref, cap):
    units, wide = weight_ref.shape[1:]
    me = place_in_half(half)
    acts = jnp.concatenate([recv_ref[me ^ r, :, wide:] for r in range(half)], axis=0)
    total = jnp.dot(acts[:, :units], weight_ref[0], preferred_element_type=f32)
    total = total + jnp.dot(acts[:, units:], beside_ref[0], preferred_element_type=f32)
    return total.astype(bf16).reshape(half // 2, 2, cap, wide)


def forward_far_body(half, recv_ref, weight_ref, beside_ref, *refs):
    out_refs, grads_ref = refs[:-1], refs[-1]
    grad_rows_body(recv_ref, weight_ref, beside_ref, grads_ref)
    total = output_rows(half, recv_ref, weight_ref, beside_ref, out_refs[0].shape[1])
    for distance, ref in enumerate(out_refs):
        ref[...] = total[distance]


def forward_own_body(half, recv_ref, weight_ref, beside_ref, grads_ref, mirror_ref, *out_refs):
    total = output_rows(half, recv_ref, weight_ref, beside_ref, out_refs[0].shape[1])
    wide = total.shape[3]
    units = grads_ref.shape[2]
    me = place_in_half(half)
    for core, out_ref in enumerate(out_refs):
        out_ref[:, :, 0:wide] = total[:, core]
        for distance in range(half // 2):
            source = me ^ (2 * distance + core)
            out_ref[distance, :, wide : wide + units] = grads_ref[source]
            out_ref[distance, :, wide + units :] = mirror_ref[source]


def grad_rows_body(recv_ref, weight_ref, beside_ref, out_ref):
    units, wide = weight_ref.shape[1:]
    scaled = rows_of(recv_ref, 0, wide)
    for part, weight in enumerate((weight_ref[0], beside_ref[0])):
        rows = lax.dot_general(
            scaled, weight, (((1,), (1,)), ((), ())), preferred_element_type=f32
        )
        out_ref[:, :, part * units : (part + 1) * units] = rows.astype(bf16).reshape(
            out_ref.shape[:2] + (units,)
        )


def join_cores_body(keep_ref, got_ref, *out_refs):
    for distance, ref in enumerate(out_refs):
        ref[0] = keep_ref[distance]
        ref[1] = got_ref[distance]


def other_core_body(*refs):
    out_ref = refs[-1]
    for distance, ref in enumerate(refs[:-1]):
        out_ref[distance] = ref[1]


def update_body(
    recv_ref, far_ref, first_ref, second_ref, first_beside, second_beside, out_ref
):
    _, units, wide = first_beside.shape
    groups = out_ref.shape[0]
    narrow = wide // 2
    each = units // groups
    for part in range(2):
        grads = None
        for ref in (recv_ref, far_ref):
            more = lax.dot_general(
                rows_of(ref, wide, 2 * units),
                rows_of(ref, part * narrow, narrow),
                (((0,), (0,)), ((), ())),
                preferred_element_type=f32,
            )
            grads = more if grads is None else grads + more
        for side in range(2):
            own = (first_ref, second_ref) if side == 0 else (first_beside, second_beside)
            moments = [ref[0, :, part * narrow : (part + 1) * narrow] for ref in own]
            grad = grads[side * units : (side + 1) * units]
            first = first_decay * moments[0].astype(f32) + (1.0 - first_decay) * grad
            second = second_decay * moments[1].astype(f32)
            second = second + (1.0 - second_decay) * grad * grad
            root = second * lax.rsqrt(second) + adam_epsilon
            step = (first * pl.reciprocal(root, approx=True)).astype(bf16)
            out_ref[:, part, side * each : (side + 1) * each, 0:narrow] = step.reshape(
                groups, each, narrow
            )


def combine_far_body(half, acts_ref, *refs):
    near_refs, other_ref, out_ref = refs[:-2], refs[-2], refs[-1]
    pieces = []
    for distance, ref in enumerate(near_refs):
        pieces += [ref[0], other_ref[distance]]
    out_ref[...] = combined(half, acts_ref, pieces, out_ref.shape[0]).astype(bf16)


def combine_own_body(half, acts_ref, chosen_ref, far_ref, *refs):
    out_ref = refs[-1]
    tok, wide = out_ref.shape
    pieces = [ref[core, :, 0:wide] for ref in refs[:-1] for core in range(2)]
    _, weights = read_meta(acts_ref)
    total = weighted_sum(chosen_ref[...], weights, jnp.concatenate(pieces, axis=0), tok)
    out_ref[...] = (total + far_ref[...].astype(f32)).astype(bf16)


def choose_body(half, acts_ref, chosen_ref):
    ids, _ = read_meta(acts_ref)
    chosen_ref[...] = returned_choice(half, ids, chosen_ref.shape[0] // half)


def returned_choice(half, ids, cap):
    level, _ = level_and_side(half)
    ids = ids.astype(jnp.int32) - half * level
    inside = (ids >= 0) & (ids < half)
    bin_of = jnp.where(inside, ids ^ place_in_half(half), -1).astype(f32)
    return slot_choice(bin_of, half, cap).astype(f32).astype(bf16)


def weighted_sum(chosen, weights, rows, tok):
    diagonal = same_index(tok)
    total = None
    for choice in range(2):
        picked = lax.dot_general(
            chosen[:, choice * tok : (choice + 1) * tok],
            rows,
            (((0,), (0,)), ((), ())),
            preferred_element_type=f32,
        )
        upright = jnp.sum(jnp.where(diagonal, weights[choice], 0.0), axis=1, keepdims=True)
        part = upright * picked
        total = part if total is None else total + part
    return total


def combined(half, acts_ref, pieces, tok):
    ids, weights = read_meta(acts_ref)
    chosen = returned_choice(half, ids, pieces[0].shape[0])
    return weighted_sum(chosen, weights, jnp.concatenate(pieces, axis=0), tok)


def pick_grads_body(half, meta_ref, *refs):
    near_refs, own_ref, send_ref = refs[:-2], refs[-2], refs[-1]
    units = own_ref.shape[1]
    _, cap, total_wide = near_refs[0].shape
    wide = total_wide - 4 * units
    level, _ = level_and_side(half)
    ids, _ = read_meta(meta_ref)
    upper = (ids >= half).astype(jnp.int32)
    place = (ids.astype(jnp.int32) - half * upper) ^ place_in_half(half)
    bin_of = (2 * place + (upper ^ level)).astype(f32)
    chosen = slot_choice(bin_of, 2 * half, cap).astype(f32).astype(bf16)
    for part, out_ref in enumerate((own_ref, send_ref)):
        pieces = []
        for ref in near_refs:
            for core in range(2):
                for expert in range(2):
                    at = wide + (2 * expert + part) * units
                    pieces.append(ref[core, :, at : at + units])
        picked = lax.dot_general(
            chosen,
            jnp.concatenate(pieces, axis=0),
            (((0,), (0,)), ((), ())),
            preferred_element_type=f32,
        )
        out_ref[...] = picked.astype(out_ref.dtype)


def gate_grads_body(acts_ref, own_ref, got_ref, out_ref):
    tok = acts_ref.shape[0]
    units = own_ref.shape[1]
    for choice in range(2):
        at = 2 * choice * units
        lines = slice(choice * tok, (choice + 1) * tok)
        gate = acts_ref[:, at : at + units].astype(f32)
        up = acts_ref[:, at + units : at + 2 * units].astype(f32)
        grad = own_ref[lines, :] + got_ref[lines, :].astype(f32)
        sigmoid = jax.nn.sigmoid(gate)
        out_ref[:, at : at + units] = (
            grad * up * sigmoid * (1.0 + gate * (1.0 - sigmoid))
        ).astype(bf16)
        out_ref[:, at + units : at + 2 * units] = (grad * (gate * sigmoid)).astype(bf16)


def route_steps_body(source_ref, line_ref, recv_ref, out_ref):
    count, each, wide = out_ref.shape
    for k in range(count):
        line = pl.multiple_of(line_ref[k] * each, each)
        out_ref[k] = recv_ref[source_ref[k], pl.ds(line, each), 0:wide]


def place_steps_body(recv_ref, out_ref):
    groups, parts, sides, each, wide = recv_ref.shape
    for group in range(groups):
        for part in range(parts):
            for side in range(sides):
                at = (side * parts + part) * wide
                out_ref[group * each : (group + 1) * each, at : at + wide] = recv_ref[
                    group, part, side
                ]


def after(x, *others):
    return lax.optimization_barrier((x, *others))[0]


def mirrored_local(
    swap_pairs,
    expert_ids,
    route_weights,
    gate_up,
    grad_out,
    down_weight,
    first_moment,
    second_moment,
):
    places = lax.axis_size("expert")
    half = places // 2
    level, side = level_and_side(half)
    tok, top = expert_ids.shape
    units = down_weight.shape[1]
    wide = grad_out.shape[1]
    narrow = wide // 2
    cap = 2 * tok * top // places
    each = units // half
    across = [(k, (k + half) % places) for k in range(places)]
    beside = [(0, 1), (1, 0)]
    diagonal = [
        (2 * k + a, 2 * ((k + half) % places) + 1 - a) for k in range(places) for a in range(2)
    ]
    groups = [list(range(half)), list(range(half, places))]

    def mirror(x):
        return lax.ppermute(x, "expert", across)

    def neighbour(x):
        return lax.ppermute(x, "hidden", beside)

    def exchange(x):
        return lax.all_to_all(
            x, "expert", split_axis=0, concat_axis=0, tiled=True, axis_index_groups=groups
        )

    def shaped(*shape, dtype=bf16):
        return jax.ShapeDtypeStruct(shape, dtype)

    grads_far = [mirror(grad_out)]
    acts = gate_up.reshape(tok, 4 * units)
    hidden, noted = whole_call(
        prepare_body, (shaped(top * tok, units), shaped(top * tok + 16, units)), "prepare"
    )(acts, jnp.concatenate([expert_ids.astype(f32), route_weights], axis=1))
    noted_far = mirror(noted)
    hidden_beside = neighbour(hidden)
    hidden_diagonal = lax.ppermute(hidden, ("expert", "hidden"), diagonal)

    split = whole_call(split_body, (shaped(1, units, wide),) * 2, "split_state")
    weight, weight_other = split(down_weight[0])
    first, first_other = split(after(first_moment[0], hidden))
    second, second_other = split(after(second_moment[0], hidden))
    weight_beside = neighbour(weight_other)
    first_beside = neighbour(first_other)
    second_beside = neighbour(second_other)

    row = wide + 2 * units
    pack = functools.partial(
        whole_call, functools.partial(pack_body, half), shaped(half, cap, row)
    )
    packed = pack("pack_own")(noted, hidden_beside, grad_out)
    recv = exchange(packed)

    packed_far = pack("pack_far", moved=HEAVY)(noted_far, hidden_diagonal, *grads_far)
    recv, packed_far, weight_beside, first_beside = lax.optimization_barrier(
        (recv, packed_far, weight_beside, first_beside)
    )
    recv_far = exchange(packed_far)
    grad_rows = whole_call(grad_rows_body, shaped(half, cap, 2 * units), "grad_rows")
    rows_own = grad_rows(recv, weight, weight_beside)
    recv_far, second_beside, rows_own = lax.optimization_barrier(
        (recv_far, second_beside, rows_own)
    )

    def at_distance(x, distance):
        return lax.ppermute(x, "expert", [(k, k ^ distance) for k in range(places)])

    def by_chip(outputs):
        return [outputs[0]] + [at_distance(outputs[k], 2 * k) for k in range(1, half // 2)]

    pairs = (shaped(2, cap, wide),) * (half // 2)
    extended = wide + 4 * units
    *outputs_far, rows_send = whole_call(
        functools.partial(forward_far_body, half),
        pairs + (shaped(half, cap, 2 * units),),
        "forward_far",
    )(recv_far, weight, weight_beside)

    rows_mirror = mirror(rows_send)
    steps = whole_call(update_body, shaped(half, 2, 2 * each, narrow), "update")(
        recv, after(recv_far, rows_send), first, second, first_beside, second_beside
    )
    spread = lax.all_to_all(
        steps.reshape(places, 2 * each, narrow),
        "expert",
        split_axis=0,
        concat_axis=0,
        tiled=True,
    )

    near_far = by_chip(outputs_far)
    near_far, rows_mirror = lax.optimization_barrier((near_far, rows_mirror, steps))[:2]
    crossing = whole_call(
        other_core_body, shaped(half // 2, cap, wide), "other_core_far"
    )(*near_far)
    combined_send = whole_call(
        functools.partial(combine_far_body, half), shaped(tok, wide), "combine_far", 55_000_000
    )(noted_far, *near_far, at_distance(crossing, 1))
    combined_far = mirror(combined_send)
    keep_core, send_core = whole_call(
        functools.partial(forward_own_body, half),
        (shaped(half // 2, cap, extended),) * 2,
        "forward_own",
    )(after(recv, combined_send), weight, weight_beside, rows_own, rows_mirror)
    joined = whole_call(join_cores_body, (shaped(2, cap, extended),) * (half // 2), "join_cores")(
        keep_core, at_distance(send_core, 1)
    )
    near = by_chip(joined)

    partner = partner_table(swap_pairs, places)
    sides = jnp.tile(jnp.arange(2, dtype=jnp.int32), places)
    smem = pl.BlockSpec(memory_space=pltpu.SMEM)
    vmem = pl.BlockSpec(memory_space=pltpu.VMEM)
    routed = pl.pallas_call(
        route_steps_body,
        in_specs=[smem, smem, vmem],
        out_specs=vmem,
        out_shape=shaped(2 * places, each, narrow),
        name="route_steps",
        compiler_params=KERNEL_PARAMS,
    )(jnp.repeat(partner, 2).astype(jnp.int32), (sides ^ side).astype(jnp.int32), spread)
    placed = lax.all_to_all(
        after(routed, combined_send), ("expert", "hidden"), split_axis=0, concat_axis=0, tiled=True
    )

    chosen = whole_call(
        functools.partial(choose_body, half), shaped(half * cap, top * tok), "choose", HEAVY
    )(after(noted, spread))
    near, combined_far, chosen = lax.optimization_barrier((near, combined_far, chosen))
    grads_own, grads_send = whole_call(
        functools.partial(pick_grads_body, half),
        (shaped(top * tok, units, dtype=f32), shaped(top * tok, units)),
        "pick_grads",
    )(noted, *near)
    grad_gate_up = whole_call(gate_grads_body, shaped(tok, 4 * units), "gate_grads")(
        acts, grads_own, neighbour(grads_send)
    ).reshape(gate_up.shape)
    combined = whole_call(
        functools.partial(combine_own_body, half), shaped(tok, wide), "combine_own"
    )(noted, chosen, combined_far, *near)
    adam_step = whole_call(place_steps_body, shaped(units, 2 * wide), "place_steps")(
        placed.reshape(half, 2, 2, each, narrow)
    )
    return combined, grad_gate_up, adam_step[None]


def chosen_local(places, sides, *arrays):
    tok, top = arrays[1].shape
    units = arrays[5].shape[1]
    wide = arrays[4].shape[1]
    cap = 2 * tok * top // places
    fits = sides == 2 and top == 2 and places % 4 == 0 and places <= 256
    fits = fits and places * cap == 2 * tok * top and cap % 16 == 0
    fits = fits and wide % 256 == 0 and units == tok and tok % 128 == 0
    fits = fits and places & (places - 1) == 0 and (units // (places // 2)) % 16 == 0
    fits = fits and cap == 2 * (units // (places // 2))
    return mirrored_local(*arrays) if fits else general_local(*arrays)


def solution(mesh):
    placed = (
        P(),
        P("expert", None),
        P("expert", None),
        P("expert", None, None, "hidden"),
        P("expert", "hidden"),
        P("expert", "hidden", None),
        P("expert", "hidden", None),
        P("expert", "hidden", None),
    )
    return jax.shard_map(
        functools.partial(chosen_local, mesh.shape["expert"], mesh.shape["hidden"]),
        mesh=mesh,
        in_specs=placed,
        out_specs=(
            P("expert", "hidden"),
            P("expert", None, None, "hidden"),
            P("expert", "hidden", None),
        ),
        check_vma=False,
    )
```

```python
import functools
import jax
import jax.numpy as jnp
from jax import lax
from jax.experimental import pallas as pl
from jax.experimental.pallas import tpu as pltpu
from jax.sharding import PartitionSpec as P

first_decay = 0.9
second_decay = 0.95
adam_epsilon = 1e-08


def partner_table(swap_pairs, places):
    column = jnp.arange(places, dtype=jnp.int32)
    left = swap_pairs[:, 0]
    right = swap_pairs[:, 1]
    moved = jnp.where(left[:, None] == column[None, :], right[:, None] - column[None, :], 0)
    moved = moved + jnp.where(right[:, None] == column[None, :], left[:, None] - column[None, :], 0)
    return column + jnp.sum(moved, axis=0)


def relocate_state(weight_here, first_here, second_here, partner):
    places = partner.shape[0]
    shape_here = weight_here.shape
    spread = (
        lax.all_to_all(
            weight_here.reshape(places, -1), "expert", split_axis=0, concat_axis=0, tiled=True
        ),
        lax.all_to_all(
            first_here.reshape(places, -1), "expert", split_axis=0, concat_axis=0, tiled=True
        ),
        lax.all_to_all(
            second_here.reshape(places, -1), "expert", split_axis=0, concat_axis=0, tiled=True
        ),
    )
    ordered = tuple((jnp.take(member, partner, axis=0) for member in spread))
    collected = (
        lax.all_to_all(ordered[0], "expert", split_axis=0, concat_axis=0, tiled=True),
        lax.all_to_all(ordered[1], "expert", split_axis=0, concat_axis=0, tiled=True),
        lax.all_to_all(ordered[2], "expert", split_axis=0, concat_axis=0, tiled=True),
    )
    return tuple((member.reshape(shape_here) for member in collected))


def slot_numbers(destination, places, capacity):
    column = jnp.arange(places, dtype=jnp.int32)
    one_hot = (destination[:, None] == column[None, :]).astype(jnp.int32)
    before = jnp.cumsum(one_hot, axis=0) - one_hot
    earlier_count = jnp.sum(before * one_hot, axis=1)
    return destination * capacity + earlier_count


def general_local(
    swap_pairs,
    expert_ids,
    route_weights,
    gate_up,
    grad_out,
    down_weight,
    first_moment,
    second_moment,
):
    places = lax.axis_size("expert")
    tok_count, top_count = expert_ids.shape
    hid_dev = down_weight.shape[1]
    capacity = 2 * tok_count * top_count // places
    total_slots = places * capacity
    choice_count = tok_count * top_count
    partner = partner_table(swap_pairs, places)
    weight_here = down_weight[0]
    first_here = first_moment[0]
    second_here = second_moment[0]
    flat_ids = expert_ids.reshape(-1)
    column = jnp.arange(places, dtype=jnp.int32)
    weight_here, first_here, second_here = relocate_state(
        weight_here, first_here, second_here, partner
    )
    destination = jnp.sum(
        jnp.where(flat_ids[:, None] == column[None, :], partner[None, :], 0), axis=1
    )
    slot_index = slot_numbers(destination, places, capacity)
    choice_acts = gate_up.reshape(choice_count, 2 * hid_dev)
    scaled = (route_weights[:, :, None] * grad_out[:, None, :].astype(jnp.float32)).astype(
        jnp.bfloat16
    )
    scaled = scaled.reshape(choice_count, grad_out.shape[1])
    send_acts = jnp.zeros((total_slots, 2 * hid_dev), jnp.bfloat16).at[slot_index].set(choice_acts)
    send_grads = (
        jnp.zeros((total_slots, grad_out.shape[1]), jnp.bfloat16).at[slot_index].set(scaled)
    )
    recv_acts, recv_grads = (
        lax.all_to_all(
            send_acts.reshape(places, capacity, 2 * hid_dev),
            "expert",
            split_axis=0,
            concat_axis=0,
            tiled=True,
        ),
        lax.all_to_all(
            send_grads.reshape(places, capacity, grad_out.shape[1]),
            "expert",
            split_axis=0,
            concat_axis=0,
            tiled=True,
        ),
    )
    recv_acts = recv_acts.reshape(total_slots, 2 * hid_dev)
    recv_grads = recv_grads.reshape(total_slots, grad_out.shape[1])
    gate_pre = recv_acts[:, :hid_dev].astype(jnp.float32)
    up_pre = recv_acts[:, hid_dev:].astype(jnp.float32)
    sigmoid_gate = jax.nn.sigmoid(gate_pre)
    silu_gate = gate_pre * sigmoid_gate
    hidden = (silu_gate * up_pre).astype(jnp.bfloat16)
    partial_value = jnp.dot(hidden, weight_here, preferred_element_type=jnp.float32)
    summed = lax.psum_scatter(
        partial_value.astype(jnp.bfloat16), "hidden", scatter_dimension=1, tiled=True
    ).astype(jnp.float32)
    returned = lax.all_to_all(
        summed.reshape(places, capacity, summed.shape[1]).astype(jnp.bfloat16),
        "expert",
        split_axis=0,
        concat_axis=0,
        tiled=True,
    ).astype(jnp.float32)
    per_choice = jnp.take(returned.reshape(total_slots, summed.shape[1]), slot_index, axis=0)
    per_choice = per_choice.reshape(tok_count, top_count, summed.shape[1])
    combined = jnp.einsum("tk,tkd->td", route_weights, per_choice).astype(jnp.bfloat16)
    portion = lax.all_gather(recv_grads, "hidden", axis=1, tiled=True)
    grad_hidden = lax.dot_general(
        portion, weight_here, (((1,), (1,)), ((), ())), preferred_element_type=jnp.float32
    )
    product_block = lax.dot_general(
        hidden, portion, (((0,), (0,)), ((), ())), preferred_element_type=jnp.float32
    )
    grad_weight = product_block
    grad_hidden, grad_weight = (grad_hidden, grad_weight)
    grad_gate = grad_hidden * up_pre * sigmoid_gate * (1.0 + gate_pre * (1.0 - sigmoid_gate))
    grad_up = grad_hidden * silu_gate
    grad_rows = jnp.concatenate([grad_gate, grad_up], axis=1).astype(jnp.bfloat16)
    returned_grads = lax.all_to_all(
        grad_rows.reshape(places, capacity, 2 * hid_dev),
        "expert",
        split_axis=0,
        concat_axis=0,
        tiled=True,
    )
    grad_gate_up = jnp.take(returned_grads.reshape(total_slots, 2 * hid_dev), slot_index, axis=0)
    grad_gate_up = grad_gate_up.reshape(tok_count, top_count, 2, hid_dev)
    first_new = first_decay * first_here.astype(jnp.float32) + (1.0 - first_decay) * grad_weight
    second_new = (
        second_decay * second_here.astype(jnp.float32)
        + (1.0 - second_decay) * grad_weight * grad_weight
    )
    update = (first_new / (jnp.sqrt(second_new) + adam_epsilon)).astype(jnp.bfloat16)
    return (combined, grad_gate_up, update[None])


bf16 = jnp.bfloat16
f32 = jnp.float32
HEAVY = 10_000_000_000
KERNEL_PARAMS = pltpu.CompilerParams(vmem_limit_bytes=40 * 1024 * 1024)


def whole_call(body, out_shape, name, moved=None):
    cost = None if moved is None else pl.CostEstimate(flops=100 * moved, bytes_accessed=moved, transcendentals=0)
    return pl.pallas_call(
        body, out_shape=out_shape, name=name, compiler_params=KERNEL_PARAMS, cost_estimate=cost
    )


def level_and_side(half):
    return lax.axis_index("expert") // half, lax.axis_index("hidden")


def columns_at(ref, index, wide):
    return ref[:, pl.ds(pl.multiple_of(index * wide, wide), wide)]


def same_index(size):
    first = lax.broadcasted_iota(jnp.int32, (size, size), 0)
    second = lax.broadcasted_iota(jnp.int32, (size, size), 1)
    return first == second


def prepare_body(acts_ref, choices_ref, hidden_ref, far_ref):
    tok = acts_ref.shape[0]
    units = acts_ref.shape[1] // 4
    for choice in range(2):
        at = 2 * choice * units
        gate = acts_ref[:, at : at + units].astype(f32)
        up = acts_ref[:, at + units : at + 2 * units].astype(f32)
        value = (gate * jax.nn.sigmoid(gate) * up).astype(bf16)
        hidden_ref[choice * tok : (choice + 1) * tok, :] = value
        far_ref[choice * tok : (choice + 1) * tok, :] = value
    ids, weights = choices_ref[:, 0:2], choices_ref[:, 2:4]
    high = weights.astype(bf16)
    middle = (weights - high.astype(f32)).astype(bf16)
    low = (weights - high.astype(f32) - middle.astype(f32)).astype(bf16)
    unit = same_index(tok).astype(f32).astype(bf16)
    pieces = [
        lax.dot_general(piece, unit, (((0,), (0,)), ((), ())), preferred_element_type=f32)
        for piece in (ids.astype(bf16), high, middle, low)
    ]
    blank = jnp.zeros((16 - 8, tok), f32)
    far_ref[2 * tok : 2 * tok + 16, :] = jnp.concatenate(pieces + [blank], axis=0).astype(bf16)


def split_body(ref, keep_ref, other_ref):
    side = lax.axis_index("hidden")
    wide = ref.shape[1] // 2
    keep_ref[0] = columns_at(ref, side, wide)
    other_ref[0] = columns_at(ref, 1 - side, wide)


def read_meta(ref):
    tok = ref.shape[1]
    meta = ref[2 * tok : 2 * tok + 16, :].astype(f32)
    ids = jnp.concatenate([meta[0:1, :], meta[1:2, :]], axis=1)
    weights = [
        meta[2 + k : 3 + k, :] + meta[4 + k : 5 + k, :] + meta[6 + k : 7 + k, :] for k in range(2)
    ]
    return ids, weights


def slot_choice(bin_of, bins, cap):
    count = bin_of.shape[1]
    column = lax.broadcasted_iota(jnp.int32, (bins, count), 0).astype(f32)
    one_hot = (bin_of == column).astype(f32)
    first = lax.broadcasted_iota(jnp.int32, (count, count), 0)
    second = lax.broadcasted_iota(jnp.int32, (count, count), 1)
    earlier = (first < second).astype(f32).astype(bf16)
    rank = jnp.dot(one_hot.astype(bf16), earlier, preferred_element_type=f32)
    slot = jnp.sum(one_hot * (rank + column * cap + 1.0), axis=0, keepdims=True) - 1.0
    return slot == lax.broadcasted_iota(jnp.int32, (bins * cap, count), 0).astype(f32)


def pack_body(half, acts_ref, beside_ref, *refs):
    out_ref = refs[-1]
    bins, cap, _ = out_ref.shape
    units = beside_ref.shape[1]
    grads = jnp.concatenate([ref[...] for ref in refs[:-1]], axis=0)
    tok, wide = grads.shape
    level, _ = level_and_side(half)
    ids, weights = read_meta(acts_ref)
    chosen = slot_choice(ids - (half * level).astype(f32), bins, cap)
    weights = jnp.concatenate(weights, axis=1)
    factor = jnp.sum(jnp.where(chosen, weights, 0.0), axis=1, keepdims=True)
    one_hot = chosen.astype(f32)
    by_token = (one_hot[:, :tok] + one_hot[:, tok:]).astype(bf16)
    rows = jnp.dot(by_token, grads, preferred_element_type=f32)
    out_ref[:, :, 0:wide] = (rows * factor).astype(bf16).reshape(bins, cap, wide)
    for side in range((out_ref.shape[2] - wide) // units):
        ref = (acts_ref, beside_ref)[side]
        at = wide + side * units
        acts = jnp.dot(
            one_hot.astype(bf16), ref[0 : 2 * tok, :], preferred_element_type=f32
        )
        out_ref[:, :, at : at + units] = acts.astype(bf16).reshape(bins, cap, units)


def rows_of(ref, start, size):
    sources, cap, _ = ref.shape
    return ref[:, :, start : start + size].reshape(sources * cap, size)


def place_in_half(half):
    return lax.rem(lax.axis_index("expert"), half)


def output_rows(half, recv_refs, weight_ref, beside_ref, cap):
    units, wide = weight_ref.shape[1:]
    me = place_in_half(half)
    total = None
    for ref, at, weight in zip(recv_refs, (wide, recv_refs[1].shape[2] - units), (weight_ref, beside_ref)):
        acts = jnp.concatenate([ref[me ^ r, :, at : at + units] for r in range(half)], axis=0)
        part = jnp.dot(acts, weight[0], preferred_element_type=f32)
        total = part if total is None else total + part
    return total.astype(bf16).reshape(half // 2, 2, cap, wide)


def forward_far_body(half, recv_ref, weight_ref, beside_ref, *refs):
    out_refs, grads_ref = refs[:-1], refs[-1]
    grad_rows_body(recv_ref, weight_ref, beside_ref, grads_ref)
    total = output_rows(half, (recv_ref,) * 2, weight_ref, beside_ref, out_refs[0].shape[1])
    for distance, ref in enumerate(out_refs):
        ref[...] = total[distance]


def forward_own_body(half, recv_ref, acts_ref, weight_ref, beside_ref, grads_ref, mirror_ref, *out_refs):
    total = output_rows(
        half, (recv_ref, acts_ref), weight_ref, beside_ref, out_refs[0].shape[1]
    )
    wide = total.shape[3]
    units = grads_ref.shape[2]
    me = place_in_half(half)
    for core, out_ref in enumerate(out_refs):
        out_ref[:, :, 0:wide] = total[:, core]
        for distance in range(half // 2):
            source = me ^ (2 * distance + core)
            out_ref[distance, :, wide : wide + units] = grads_ref[source]
            out_ref[distance, :, wide + units :] = mirror_ref[source]


def grad_rows_body(recv_ref, weight_ref, beside_ref, out_ref):
    units, wide = weight_ref.shape[1:]
    scaled = rows_of(recv_ref, 0, wide)
    for part, weight in enumerate((weight_ref[0], beside_ref[0])):
        rows = lax.dot_general(
            scaled, weight, (((1,), (1,)), ((), ())), preferred_element_type=f32
        )
        out_ref[:, :, part * units : (part + 1) * units] = rows.astype(bf16).reshape(
            out_ref.shape[:2] + (units,)
        )


def join_cores_body(keep_ref, got_ref, *out_refs):
    for distance, ref in enumerate(out_refs):
        ref[0] = keep_ref[distance]
        ref[1] = got_ref[distance]


def other_core_body(*refs):
    out_ref = refs[-1]
    for distance, ref in enumerate(refs[:-1]):
        out_ref[distance] = ref[1]


def update_body(
    recv_ref, acts_ref, far_ref, first_ref, second_ref, first_beside, second_beside, out_ref
):
    _, units, wide = first_beside.shape
    groups = out_ref.shape[0]
    narrow = wide // 2
    each = units // groups
    for part in range(2):
        grads = None
        own = jnp.concatenate([rows_of(recv_ref, wide, units), rows_of(acts_ref, 0, units)], axis=1)
        for ref, acts in ((recv_ref, own), (far_ref, rows_of(far_ref, wide, 2 * units))):
            more = lax.dot_general(
                acts,
                rows_of(ref, part * narrow, narrow),
                (((0,), (0,)), ((), ())),
                preferred_element_type=f32,
            )
            grads = more if grads is None else grads + more
        for side in range(2):
            own = (first_ref, second_ref) if side == 0 else (first_beside, second_beside)
            moments = [ref[0, :, part * narrow : (part + 1) * narrow] for ref in own]
            grad = grads[side * units : (side + 1) * units]
            first = first_decay * moments[0].astype(f32) + (1.0 - first_decay) * grad
            second = second_decay * moments[1].astype(f32)
            second = second + (1.0 - second_decay) * grad * grad
            root = second * lax.rsqrt(second) + adam_epsilon
            step = (first * pl.reciprocal(root, approx=True)).astype(bf16)
            out_ref[:, part, side * each : (side + 1) * each, 0:narrow] = step.reshape(
                groups, each, narrow
            )


def combine_far_body(half, acts_ref, *refs):
    near_refs, other_ref, out_ref = refs[:-2], refs[-2], refs[-1]
    pieces = []
    for distance, ref in enumerate(near_refs):
        pieces += [ref[0], other_ref[distance]]
    out_ref[...] = combined(half, acts_ref, pieces, out_ref.shape[0]).astype(bf16)


def combine_own_body(half, acts_ref, chosen_ref, far_ref, *refs):
    out_ref = refs[-1]
    tok, wide = out_ref.shape
    pieces = [ref[core, :, 0:wide] for ref in refs[:-1] for core in range(2)]
    _, weights = read_meta(acts_ref)
    total = weighted_sum(chosen_ref[...], weights, jnp.concatenate(pieces, axis=0), tok)
    out_ref[...] = (total + far_ref[...].astype(f32)).astype(bf16)


def choose_body(half, acts_ref, chosen_ref):
    ids, _ = read_meta(acts_ref)
    chosen_ref[...] = returned_choice(half, ids, chosen_ref.shape[0] // half)


def returned_choice(half, ids, cap):
    level, _ = level_and_side(half)
    ids = ids.astype(jnp.int32) - half * level
    inside = (ids >= 0) & (ids < half)
    bin_of = jnp.where(inside, ids ^ place_in_half(half), -1).astype(f32)
    return slot_choice(bin_of, half, cap).astype(f32).astype(bf16)


def weighted_sum(chosen, weights, rows, tok):
    diagonal = same_index(tok)
    total = None
    for choice in range(2):
        picked = lax.dot_general(
            chosen[:, choice * tok : (choice + 1) * tok],
            rows,
            (((0,), (0,)), ((), ())),
            preferred_element_type=f32,
        )
        upright = jnp.sum(jnp.where(diagonal, weights[choice], 0.0), axis=1, keepdims=True)
        part = upright * picked
        total = part if total is None else total + part
    return total


def combined(half, acts_ref, pieces, tok):
    ids, weights = read_meta(acts_ref)
    chosen = returned_choice(half, ids, pieces[0].shape[0])
    return weighted_sum(chosen, weights, jnp.concatenate(pieces, axis=0), tok)


def pick_grads_body(half, meta_ref, *refs):
    near_refs, own_ref, send_ref = refs[:-2], refs[-2], refs[-1]
    units = own_ref.shape[1]
    _, cap, total_wide = near_refs[0].shape
    wide = total_wide - 4 * units
    level, _ = level_and_side(half)
    ids, _ = read_meta(meta_ref)
    upper = (ids >= half).astype(jnp.int32)
    place = (ids.astype(jnp.int32) - half * upper) ^ place_in_half(half)
    bin_of = (2 * place + (upper ^ level)).astype(f32)
    chosen = slot_choice(bin_of, 2 * half, cap).astype(f32).astype(bf16)
    for part, out_ref in enumerate((own_ref, send_ref)):
        pieces = []
        for ref in near_refs:
            for core in range(2):
                for expert in range(2):
                    at = wide + (2 * expert + part) * units
                    pieces.append(ref[core, :, at : at + units])
        picked = lax.dot_general(
            chosen,
            jnp.concatenate(pieces, axis=0),
            (((0,), (0,)), ((), ())),
            preferred_element_type=f32,
        )
        out_ref[...] = picked.astype(out_ref.dtype)


def gate_grads_body(acts_ref, own_ref, got_ref, out_ref):
    tok = acts_ref.shape[0]
    units = own_ref.shape[1]
    for choice in range(2):
        at = 2 * choice * units
        lines = slice(choice * tok, (choice + 1) * tok)
        gate = acts_ref[:, at : at + units].astype(f32)
        up = acts_ref[:, at + units : at + 2 * units].astype(f32)
        grad = own_ref[lines, :] + got_ref[lines, :].astype(f32)
        sigmoid = jax.nn.sigmoid(gate)
        out_ref[:, at : at + units] = (
            grad * up * sigmoid * (1.0 + gate * (1.0 - sigmoid))
        ).astype(bf16)
        out_ref[:, at + units : at + 2 * units] = (grad * (gate * sigmoid)).astype(bf16)


def route_steps_body(source_ref, line_ref, recv_ref, out_ref):
    count, each, wide = out_ref.shape
    for k in range(count):
        line = pl.multiple_of(line_ref[k] * each, each)
        out_ref[k] = recv_ref[source_ref[k], pl.ds(line, each), 0:wide]


def place_steps_body(recv_ref, out_ref):
    groups, parts, sides, each, wide = recv_ref.shape
    for group in range(groups):
        for part in range(parts):
            for side in range(sides):
                at = (side * parts + part) * wide
                out_ref[group * each : (group + 1) * each, at : at + wide] = recv_ref[
                    group, part, side
                ]


def after(x, *others):
    return lax.optimization_barrier((x, *others))[0]


def mirrored_local(
    swap_pairs,
    expert_ids,
    route_weights,
    gate_up,
    grad_out,
    down_weight,
    first_moment,
    second_moment,
):
    places = lax.axis_size("expert")
    half = places // 2
    level, side = level_and_side(half)
    tok, top = expert_ids.shape
    units = down_weight.shape[1]
    wide = grad_out.shape[1]
    narrow = wide // 2
    cap = 2 * tok * top // places
    each = units // half
    across = [(k, (k + half) % places) for k in range(places)]
    beside = [(0, 1), (1, 0)]
    diagonal = [
        (2 * k + a, 2 * ((k + half) % places) + 1 - a) for k in range(places) for a in range(2)
    ]
    groups = [list(range(half)), list(range(half, places))]

    def mirror(x):
        return lax.ppermute(x, "expert", across)

    def neighbour(x):
        return lax.ppermute(x, "hidden", beside)

    def exchange(x):
        return lax.all_to_all(
            x, "expert", split_axis=0, concat_axis=0, tiled=True, axis_index_groups=groups
        )

    def shaped(*shape, dtype=bf16):
        return jax.ShapeDtypeStruct(shape, dtype)

    grads_far = [mirror(grad_out)]
    acts = gate_up.reshape(tok, 4 * units)
    hidden, noted = whole_call(
        prepare_body, (shaped(top * tok, units), shaped(top * tok + 16, units)), "prepare"
    )(acts, jnp.concatenate([expert_ids.astype(f32), route_weights], axis=1))
    noted_far = mirror(noted)
    hidden_diagonal = lax.ppermute(hidden, ("expert", "hidden"), diagonal)

    split = whole_call(split_body, (shaped(1, units, wide),) * 2, "split_state")
    weight, weight_other = split(down_weight[0])
    first, first_other = split(after(first_moment[0], hidden))
    second, second_other = split(after(second_moment[0], hidden))
    weight_beside = neighbour(weight_other)
    first_beside = neighbour(first_other)
    second_beside = neighbour(second_other)

    row = wide + 2 * units
    pack = functools.partial(whole_call, functools.partial(pack_body, half))
    packed = pack(shaped(half, cap, wide + units), "pack_own")(
        after(noted, weight_other, first_other), hidden, grad_out
    )
    recv = exchange(packed)
    acts_beside = neighbour(recv[:, :, wide:])

    packed_far = pack(shaped(half, cap, row), "pack_far", moved=HEAVY)(noted_far, hidden_diagonal, *grads_far)
    recv, packed_far, weight_beside, first_beside = lax.optimization_barrier(
        (recv, packed_far, weight_beside, first_beside)
    )
    recv_far = exchange(packed_far)
    grad_rows = whole_call(grad_rows_body, shaped(half, cap, 2 * units), "grad_rows")
    rows_own = grad_rows(recv, weight, weight_beside)
    recv_far, second_beside, rows_own, acts_beside = lax.optimization_barrier(
        (recv_far, second_beside, rows_own, acts_beside)
    )

    def at_distance(x, distance):
        return lax.ppermute(x, "expert", [(k, k ^ distance) for k in range(places)])

    def by_chip(outputs):
        return [outputs[0]] + [at_distance(outputs[k], 2 * k) for k in range(1, half // 2)]

    pairs = (shaped(2, cap, wide),) * (half // 2)
    extended = wide + 4 * units
    *outputs_far, rows_send = whole_call(
        functools.partial(forward_far_body, half),
        pairs + (shaped(half, cap, 2 * units),),
        "forward_far",
    )(recv_far, weight, weight_beside)

    rows_mirror = mirror(rows_send)
    steps = whole_call(update_body, shaped(half, 2, 2 * each, narrow), "update")(
        recv, acts_beside, after(recv_far, rows_send), first, second, first_beside, second_beside
    )
    spread = lax.all_to_all(
        steps.reshape(places, 2 * each, narrow),
        "expert",
        split_axis=0,
        concat_axis=0,
        tiled=True,
    )

    near_far = by_chip(outputs_far)
    near_far, rows_mirror = lax.optimization_barrier((near_far, rows_mirror, steps))[:2]
    crossing = whole_call(
        other_core_body, shaped(half // 2, cap, wide), "other_core_far"
    )(*near_far)
    combined_send = whole_call(
        functools.partial(combine_far_body, half), shaped(tok, wide), "combine_far", 55_000_000
    )(noted_far, *near_far, at_distance(crossing, 1))
    combined_far = mirror(combined_send)
    keep_core, send_core = whole_call(
        functools.partial(forward_own_body, half),
        (shaped(half // 2, cap, extended),) * 2,
        "forward_own",
    )(after(recv, combined_send), acts_beside, weight, weight_beside, rows_own, rows_mirror)
    joined = whole_call(join_cores_body, (shaped(2, cap, extended),) * (half // 2), "join_cores")(
        keep_core, at_distance(send_core, 1)
    )
    near = by_chip(joined)

    partner = partner_table(swap_pairs, places)
    sides = jnp.tile(jnp.arange(2, dtype=jnp.int32), places)
    smem = pl.BlockSpec(memory_space=pltpu.SMEM)
    vmem = pl.BlockSpec(memory_space=pltpu.VMEM)
    routed = pl.pallas_call(
        route_steps_body,
        in_specs=[smem, smem, vmem],
        out_specs=vmem,
        out_shape=shaped(2 * places, each, narrow),
        name="route_steps",
        compiler_params=KERNEL_PARAMS,
    )(jnp.repeat(partner, 2).astype(jnp.int32), (sides ^ side).astype(jnp.int32), spread)
    placed = lax.all_to_all(
        after(routed, combined_send), ("expert", "hidden"), split_axis=0, concat_axis=0, tiled=True
    )

    chosen = whole_call(
        functools.partial(choose_body, half), shaped(half * cap, top * tok), "choose", HEAVY
    )(after(noted, spread))
    near, combined_far, chosen = lax.optimization_barrier((near, combined_far, chosen))
    grads_own, grads_send = whole_call(
        functools.partial(pick_grads_body, half),
        (shaped(top * tok, units, dtype=f32), shaped(top * tok, units)),
        "pick_grads",
    )(noted, *near)
    grad_gate_up = whole_call(gate_grads_body, shaped(tok, 4 * units), "gate_grads")(
        acts, grads_own, neighbour(grads_send)
    ).reshape(gate_up.shape)
    combined = whole_call(
        functools.partial(combine_own_body, half), shaped(tok, wide), "combine_own"
    )(noted, chosen, combined_far, *near)
    adam_step = whole_call(place_steps_body, shaped(units, 2 * wide), "place_steps")(
        placed.reshape(half, 2, 2, each, narrow)
    )
    return combined, grad_gate_up, adam_step[None]


def chosen_local(places, sides, *arrays):
    tok, top = arrays[1].shape
    units = arrays[5].shape[1]
    wide = arrays[4].shape[1]
    cap = 2 * tok * top // places
    fits = sides == 2 and top == 2 and places % 4 == 0 and places <= 256
    fits = fits and places * cap == 2 * tok * top and cap % 16 == 0
    fits = fits and wide % 256 == 0 and units == tok and tok % 128 == 0
    fits = fits and places & (places - 1) == 0 and (units // (places // 2)) % 16 == 0
    fits = fits and cap == 2 * (units // (places // 2))
    return mirrored_local(*arrays) if fits else general_local(*arrays)


def solution(mesh):
    placed = (
        P(),
        P("expert", None),
        P("expert", None),
        P("expert", None, None, "hidden"),
        P("expert", "hidden"),
        P("expert", "hidden", None),
        P("expert", "hidden", None),
        P("expert", "hidden", None),
    )
    return jax.shard_map(
        functools.partial(chosen_local, mesh.shape["expert"], mesh.shape["hidden"]),
        mesh=mesh,
        in_specs=placed,
        out_specs=(
            P("expert", "hidden"),
            P("expert", None, None, "hidden"),
            P("expert", "hidden", None),
        ),
        check_vma=False,
    )
```
